32 devices in a mesh: gal: 8 (over z, y), qry: 4 (over x, core).
Axes of the slice: x: 2, y: 2, z: 4, core: 2. Of those that a mesh axis runs over, the one named last changes fastest.
Arguments:
- descriptors: bfloat16 [16384, 512], P('gal'), may hold values from -6 to 6
- query_descriptors: bfloat16 [512, 512], P('qry'), may hold values from -6 to 6
- tile_blocks: int32 [512, 2], P('gal'), may hold values from 0 to 127, as said below
- neighbours: int32 [512, 12, 128], P('gal'), may hold values from 0 to 127
Outputs:
- ranking: float32 [16384, 512], P('gal', 'qry')
- residual: float32 [16384, 512], P('gal', 'qry')
The draws below stay inside these ranges and needn't reach their ends.
Inputs may be any that keep to these rules, and one draw needn't show every extreme that they name: `tile_blocks`: every tile of the rows of one index of gal (tiles i * 64 to (i + 1) * 64 - 1 for index i) has its block row among that index's blocks i * 16 .. (i + 1) * 16 - 1, and its block column among the blocks of that index and of the two indices beside it, (i - 1) * 16 to (i + 2) * 16 - 1 within 0 to 127. A tile may be listed twice.
All inputs are finite; a program needn't handle non-finite values.
Results may differ from the reference program's by a relative error of at most 0.0003.
Values may be sent and summed in bfloat16 or wider, within the bound.
A program may use at most 128 MiB of HBM per device.

```python
import math
import jax
import jax.numpy as jnp
from jax import lax

D = 512
BLK = 128
KT = 12
QUERIES = 512
ITERS = 3
BLK_DEV = 16
TILE_DEV = 64
NB = 128
NG = 16384
TILES = 512


def draw_tile_blocks(key, part):
    key = jax.random.fold_in(key, 7)
    key_rows, key_cols = jax.random.split(key)
    place = jnp.arange(TILES, dtype=jnp.int32)
    owner = place // TILE_DEV
    slot = place % TILE_DEV
    first = owner * BLK_DEV
    lowest = jnp.maximum(0, first - BLK_DEV)
    highest = jnp.minimum(NB, first + 2 * BLK_DEV)
    rows = first + jax.random.randint(key_rows, (TILES,), 0, BLK_DEV)
    cols = jax.random.randint(key_cols, (TILES,), lowest, highest)
    rows = jnp.where(slot == 0, first, jnp.where(slot == 1, first + BLK_DEV - 1, rows))
    cols = jnp.where(slot == 0, first, jnp.where(slot == 1, highest - 1, cols))
    return jnp.stack([rows, cols], axis=1).astype(jnp.int32)


def plant(drawn, stream_key, smallest, top_value):
    spot = [jax.random.randint(jax.random.fold_in(stream_key, axis), (), 0, length) for axis, length in enumerate(drawn.shape)]
    main_axis = drawn.shape.index(max(drawn.shape))
    next_to = spot[:main_axis] + [(spot[main_axis] + 1) % drawn.shape[main_axis]] + spot[main_axis + 1:]
    return drawn.at[tuple(spot)].set(smallest).at[tuple(next_to)].set(top_value)


def level_of(rng, dims, pieces, least, high):
    loudness = 1.0
    for axis_at, shards_of in pieces:
        steps = jax.random.uniform(jax.random.fold_in(jax.random.fold_in(rng, 6), axis_at), (shards_of,), jnp.float32, least / len(pieces), high / len(pieces))
        loudness = loudness * jnp.repeat(jnp.exp(steps), dims[axis_at] // shards_of).reshape((-1,) + (1,) * (len(dims) - 1 - axis_at))
    return loudness


def centred(rng, extent, width, limit, pieces=(), kind=jnp.bfloat16):
    result = jax.random.normal(rng, extent, jnp.float32) * width
    if len(pieces) > 0:
        result = level_of(rng, extent, pieces, -0.22, 0.18) * result
    return jnp.clip(result, min=-limit, max=limit).astype(kind)


def setup_inputs(seed: int = 0) -> dict:
    keys = jax.random.split(jax.random.key(seed), 5)
    descriptors = centred(keys[0], (NG, D), 1.0, 6.0, ((0, 8),))
    query_descriptors = centred(keys[1], (QUERIES, D), 1.0, 6.0, ((0, 4),))
    tile_blocks = draw_tile_blocks(jax.random.fold_in(keys[4], 71), 0)
    neighbours = plant(jax.random.randint(keys[3], (TILES, KT, BLK), 0, BLK), jax.random.fold_in(keys[3], 1), 0, BLK - 1).astype(jnp.int32)
    return {"descriptors": descriptors, "query_descriptors": query_descriptors, "tile_blocks": tile_blocks, "neighbours": neighbours}


damping = 0.99

def build_tiles(desc_blocks, rows, cols, neighbours):
    left = desc_blocks[rows].astype(jnp.float32)
    right = desc_blocks[cols].astype(jnp.float32)
    dots = jnp.einsum('tid,tjd->tij', left, right, precision=lax.Precision.HIGHEST)
    positions = jnp.arange(BLK, dtype=jnp.int32)
    counted = jnp.zeros(dots.shape, jnp.float32)
    for entry in range(KT):
        counted = counted + (neighbours[:, entry, :, None] == positions[None, None, :]).astype(jnp.float32)
    return counted * jax.nn.softplus(dots / math.sqrt(D))

def reference(descriptors, query_descriptors, tile_blocks, neighbours):
    desc_blocks = descriptors.reshape(NB, BLK, D)
    rows = tile_blocks[:, 0]
    cols = tile_blocks[:, 1]
    tiles = build_tiles(desc_blocks, rows, cols, neighbours)
    degree = 1.0 + (jax.ops.segment_sum(lax.optimization_barrier(jnp.sum(tiles, axis=2)), rows, NB) + jax.ops.segment_sum(lax.optimization_barrier(jnp.sum(tiles, axis=1)), cols, NB)).reshape(NG)
    scale = 1.0 / jnp.sqrt(degree)

    def operate(field):
        scaled = (field * scale[:, None]).reshape(NB, BLK, QUERIES)
        forward = jnp.einsum('tij,tjq->tiq', tiles, scaled[cols], precision=lax.Precision.HIGHEST)
        backward = jnp.einsum('tij,tiq->tjq', tiles, scaled[rows], precision=lax.Precision.HIGHEST)
        total = jax.ops.segment_sum(forward, rows, NB) + jax.ops.segment_sum(backward, cols, NB)
        return field - damping * scale[:, None] * total.reshape(NG, QUERIES)
    seeds = jax.nn.softplus(jnp.dot(descriptors, query_descriptors.T, preferred_element_type=jnp.float32) / math.sqrt(D))
    ranking = jnp.zeros_like(seeds)
    residual = seeds
    direction = seeds
    norm_now = lax.optimization_barrier(jnp.sum(residual * residual, axis=0))
    for step in range(ITERS):
        image = operate(direction)
        alpha = norm_now / lax.optimization_barrier(jnp.sum(direction * image, axis=0))
        ranking = ranking + alpha * direction
        residual = residual - alpha * image
        norm_next = lax.optimization_barrier(jnp.sum(residual * residual, axis=0))
        direction = residual + norm_next / norm_now * direction
        norm_now = norm_next
    return (ranking, residual)
```

```python
import functools
import math

import jax
import jax.numpy as jnp
from jax import lax
from jax.experimental import pallas as pl
from jax.experimental.pallas import tpu as pltpu
from jax.sharding import PartitionSpec as P

BLK = 128
DAMPING = 0.99
STAGE = 4
CHUNK = 16
VMEM_LIMIT = 60 * 1024 * 1024


def softplus(value):
    return jnp.maximum(value, 0.0) + jnp.log1p(jnp.exp(-jnp.abs(value)))


def build_kernel(tiles, entries, blocks, row_ref, col_ref, window_ref, near_ref,
                 mats_ref, degree_ref, dst_ref, src_ref, count_ref, stage, sems):
    root = 1.0 / math.sqrt(window_ref.shape[1])
    degree_ref[...] = jnp.zeros_like(degree_ref)
    count_ref[0] = 0
    count_ref[1] = 0
    places = lax.broadcasted_iota(jnp.int32, (BLK, BLK), 0).astype(jnp.float32)

    def emit(mat, slot, dst, src):
        sent = count_ref[0]
        place = lax.rem(sent, STAGE)

        @pl.when(sent >= STAGE)
        def _():
            pltpu.make_async_copy(stage.at[place], mats_ref.at[0], sems.at[place]).wait()

        high = mat.astype(jnp.bfloat16)
        stage[place, :, 0:BLK] = high
        stage[place, :, BLK:] = (mat - high.astype(jnp.float32)).astype(jnp.bfloat16)
        pltpu.make_async_copy(stage.at[place], mats_ref.at[slot], sems.at[place]).start()
        count_ref[0] = sent + 1
        dst_ref[slot] = dst
        src_ref[slot] = src
        rows = pl.ds(pl.multiple_of(dst * BLK, BLK), BLK)
        degree_ref[rows, :] += jnp.broadcast_to(jnp.sum(mat, axis=1, keepdims=True), (BLK, BLK))

    def turned(t):
        left = window_ref[pl.ds(pl.multiple_of(row_ref[t] * BLK, BLK), BLK), :]
        right = window_ref[pl.ds(pl.multiple_of(col_ref[t] * BLK, BLK), BLK), :]
        dots = lax.dot_general(right, left, (((1,), (1,)), ((), ())),
                               preferred_element_type=jnp.float32)
        near = near_ref[t].astype(jnp.float32)
        counted = jnp.zeros((BLK, BLK), jnp.float32)
        for k in range(entries):
            counted += jnp.where(places == near[k:k + 1, :], 1.0, 0.0)
        return counted * softplus(dots * root)

    def mine(t):
        col = col_ref[t]
        return jnp.logical_and(col >= blocks, col < 2 * blocks)

    def emit_back(t, mat):
        slot = tiles + count_ref[1]
        emit(mat, slot, col_ref[t] - blocks, row_ref[t])
        count_ref[1] = slot - tiles + 1

    @pl.loop(0, tiles)
    def _(t):
        mat = turned(t)
        emit(mat.T, t, row_ref[t] - blocks, col_ref[t])

        @pl.when(mine(t))
        def _():
            emit_back(t, mat)

    @pl.loop(tiles, 3 * tiles)
    def _(t):
        @pl.when(mine(t))
        def _():
            emit_back(t, turned(t))

    for place in range(STAGE):
        pltpu.make_async_copy(stage.at[place], mats_ref.at[0], sems.at[place]).wait()


def build(row, col, window, near):
    total, entries, _ = near.shape
    tiles = total // 3
    blocks = window.shape[0] // (3 * BLK)
    smem = pl.BlockSpec(memory_space=pltpu.SMEM)
    vmem = pl.BlockSpec(memory_space=pltpu.VMEM)
    return pl.pallas_call(
        functools.partial(build_kernel, tiles, entries, blocks),
        out_shape=(
            jax.ShapeDtypeStruct((4 * tiles, BLK, 2 * BLK), jnp.bfloat16),
            jax.ShapeDtypeStruct((blocks * BLK, BLK), jnp.float32),
            jax.ShapeDtypeStruct((4 * tiles,), jnp.int32),
            jax.ShapeDtypeStruct((4 * tiles,), jnp.int32),
            jax.ShapeDtypeStruct((2,), jnp.int32),
        ),
        in_specs=[smem, smem, vmem, vmem],
        out_specs=(pl.BlockSpec(memory_space=pl.ANY), vmem, smem, smem, smem),
        scratch_shapes=[
            pltpu.VMEM((STAGE, BLK, 2 * BLK), jnp.bfloat16),
            pltpu.SemaphoreType.DMA((STAGE,)),
        ],
        compiler_params=pltpu.CompilerParams(vmem_limit_bytes=VMEM_LIMIT),
        name="build_tiles",
    )(row, col, window, near)


def step_kernel(step, blocks, tiles, *refs):
    refs = list(refs)

    def take(count):
        taken = refs[:count]
        del refs[:count]
        return taken

    dst_ref, src_ref, count_ref, mats_ref, scale_ref = take(5)
    if step == 0:
        dir_in, halo_in = take(2)
        res_in = dir_in
    else:
        sums_in, res_in, dir_in, image_in = take(4)
        if step == 1:
            (halo_in,) = take(1)
            tail_in = halo_in
        else:
            halo_in, tail_in = take(2)
        fresh_low, fresh_high = take(2)
    if step > 0:
        res_out, dir_out = take(2)
    image_out, sums_out = take(2)
    if step < 2:
        (send_out,) = take(1)
    if step == 1:
        halo_out, tail_out = take(2)
    mats, field, total, sems = refs

    chunks = mats.shape[0] // CHUNK
    used = tiles + count_ref[1]

    def fetch(c):
        span = pl.ds(c * CHUNK, CHUNK)
        return pltpu.make_async_copy(mats_ref.at[span], mats.at[span], sems.at[c])

    for c in range(chunks):
        @pl.when(c * CHUNK < used)
        def _():
            fetch(c).start()

    total[...] = jnp.zeros_like(total)
    sums_out[...] = jnp.zeros_like(sums_out)
    if step > 0:
        norm = sums_in[0:1, :]
        alpha = norm / sums_in[1:2, :]
        after = norm - 2.0 * alpha * sums_in[2:3, :] + alpha * alpha * sums_in[3:4, :]
        beta = after / norm

    def put(block, value):
        high = value.astype(jnp.bfloat16)
        low = (value - high.astype(jnp.float32)).astype(jnp.bfloat16)
        field[block, 0:BLK, 0:BLK] = high
        field[block, 0:BLK, BLK:] = low
        field[block, BLK:, 0:BLK] = high
        field[block, BLK:, BLK:] = low

    def rows_of(b):
        return pl.ds(pl.multiple_of(b * BLK, BLK), BLK)

    @pl.loop(0, blocks)
    def _(b):
        rows = rows_of(b)
        direction = dir_in[rows, :]
        if step > 0:
            residual = res_in[rows, :] - alpha * image_in[rows, :]
            direction = residual + beta * direction
            res_out[rows, :] = residual
            dir_out[rows, :] = direction
        put(blocks + b, direction * scale_ref[rows, :])
        for half in range(2):
            here = rows_of(half * blocks + b)
            value = halo_in[here, :]
            if step > 0:
                fresh = (fresh_low, fresh_high)[half][rows, :]
                tail = tail_in[here, :] - alpha * fresh
                value = tail + beta * value
                if step == 1:
                    halo_out[here, :] = value
                    tail_out[here, :] = tail
            put(2 * half * blocks + b, value)

    def partial(n):
        both = jnp.dot(mats[n], field[src_ref[n]], preferred_element_type=jnp.float32)
        return both[:, 0:BLK] + both[:, BLK:]

    def run(first, count):
        terms = [partial(first + i) for i in range(count)]
        for i in range(count):
            total[rows_of(dst_ref[first + i]), :] += terms[i]

    @pl.loop(0, pl.cdiv(used, CHUNK))
    def _(c):
        fetch(c).wait()
        first = c * CHUNK
        have = jnp.minimum(CHUNK, used - first)

        @pl.loop(0, have // 4)
        def _(g):
            run(first + 4 * g, 4)

        @pl.loop(have // 4 * 4, have)
        def _(i):
            run(first + i, 1)

    @pl.loop(0, blocks)
    def _(b):
        rows = rows_of(b)
        scale = scale_ref[rows, :]
        direction = (dir_out if step > 0 else dir_in)[rows, :]
        residual = (res_out if step > 0 else res_in)[rows, :]
        image = direction - DAMPING * scale * total[rows, :]
        image_out[rows, :] = image
        if step < 2:
            send_out[rows, :] = scale * image
        for place, value in enumerate(
            (residual * residual, direction * image, residual * image, image * image)
        ):
            sums_out[place:place + 1, :] += jnp.sum(value, axis=0, keepdims=True)


def run_step(step, dst, src, count, mats, scale, *rest):
    rows, columns = scale.shape[0], rest[-1].shape[1]
    tiles = dst.shape[0] // 4
    blocks = rows // BLK
    smem = pl.BlockSpec(memory_space=pltpu.SMEM)
    vmem = pl.BlockSpec(memory_space=pltpu.VMEM)
    own = jax.ShapeDtypeStruct((rows, columns), jnp.float32)
    twice = jax.ShapeDtypeStruct((2 * rows, columns), jnp.float32)
    sums = jax.ShapeDtypeStruct((8, columns), jnp.float32)
    outs = ([own, own] if step > 0 else []) + [own, sums]
    if step < 2:
        outs += [own]
    if step == 1:
        outs += [twice, twice]
    return pl.pallas_call(
        functools.partial(step_kernel, step, blocks, tiles),
        out_shape=tuple(outs),
        in_specs=[smem, smem, smem, pl.BlockSpec(memory_space=pl.ANY), vmem]
        + [vmem] * len(rest),
        out_specs=tuple(vmem for _ in outs),
        scratch_shapes=[
            pltpu.VMEM(mats.shape, jnp.bfloat16),
            pltpu.VMEM((3 * blocks, 2 * BLK, 2 * BLK), jnp.bfloat16),
            pltpu.VMEM((rows, columns), jnp.float32),
            pltpu.SemaphoreType.DMA((mats.shape[0] // CHUNK,)),
        ],
        compiler_params=pltpu.CompilerParams(vmem_limit_bytes=VMEM_LIMIT),
        name="operator_step",
    )(dst, src, count, mats, scale, *rest)


def from_sides(value):
    count = lax.axis_size("gal")
    up = [(i, i + 1) for i in range(count - 1)]
    down = [(i + 1, i) for i in range(count - 1)]
    return lax.ppermute(value, "gal", up), lax.ppermute(value, "gal", down)


def per_device(descriptors, query_descriptors, tile_blocks, neighbours):
    rows, width = descriptors.shape
    tiles = tile_blocks.shape[0]
    blocks = rows // BLK
    place = lax.axis_index("gal")
    count = lax.axis_size("gal")
    parts = lax.axis_size("qry")
    part = lax.axis_index("qry")

    def spread(value):
        size = value.shape[0] // parts
        piece = lax.dynamic_slice_in_dim(value, part * size, size, axis=0)
        pieces = jnp.stack(from_sides(piece))
        whole = lax.all_gather(pieces, "qry", axis=1)
        return whole.reshape((2,) + value.shape)

    near = neighbours.astype(jnp.bfloat16)
    beside = spread(descriptors)
    near_beside = spread(near)
    window = jnp.concatenate([beside[0], descriptors, beside[1]], axis=0)
    near_all = jnp.concatenate([near, near_beside[0], near_beside[1]], axis=0)
    below, above = from_sides(tile_blocks)
    base = (place - 1) * blocks
    far = jnp.int32(3 * blocks)
    local = jnp.concatenate([tile_blocks, below, above], axis=0) - base
    origin = jnp.repeat(jnp.array([0, -1, 1], jnp.int32), tiles) + place
    exists = jnp.logical_and(origin >= 0, origin < count)
    row = local[:, 0]
    col = jnp.where(exists, local[:, 1], far)

    mats, degree, dst, src, used = build(row, col, window, near_all)
    scale = 1.0 / jnp.sqrt(1.0 + degree)
    scale_low, scale_high = from_sides(scale[:, 0])
    seeds = jax.nn.softplus(
        lax.dot_general(window, query_descriptors, (((1,), (1,)), ((), ())),
                        preferred_element_type=jnp.float32) / math.sqrt(width)
    )
    own = seeds[rows:2 * rows]
    halo = jnp.concatenate(
        [seeds[:rows] * scale_low[:, None], seeds[2 * rows:] * scale_high[:, None]], axis=0
    )
    image0, sums0, send0 = run_step(0, dst, src, used, mats, scale, own, halo)
    fresh = from_sides(send0)
    sums0 = lax.psum(sums0, "gal")
    res1, dir1, image1, sums1, send1, halo1, tail1 = run_step(
        1, dst, src, used, mats, scale, sums0, own, own, image0, halo, *fresh
    )
    fresh = from_sides(send1)
    sums1 = lax.psum(sums1, "gal")
    res2, dir2, image2, sums2 = run_step(
        2, dst, src, used, mats, scale, sums1, res1, dir1, image1, halo1, tail1, *fresh
    )
    sums2 = lax.psum(sums2, "gal")
    alpha0, alpha1, alpha2 = (s[0:1] / s[1:2] for s in (sums0, sums1, sums2))
    ranking = alpha0 * own + alpha1 * dir1 + alpha2 * dir2
    residual = res2 - alpha2 * image2
    return ranking, residual


def solution(mesh):
    placed = (P("gal", None), P("qry", None), P("gal", None), P("gal", None, None))
    return jax.shard_map(
        per_device,
        mesh=mesh,
        in_specs=placed,
        out_specs=(P("gal", "qry"), P("gal", "qry")),
        check_vma=False,
    )
```

```python
import functools
import math

import jax
import jax.numpy as jnp
from jax import lax
from jax.experimental import pallas as pl
from jax.experimental.pallas import tpu as pltpu
from jax.sharding import PartitionSpec as P

BLK = 128
DAMPING = 0.99
STAGE = 4
CHUNK = 16
VMEM_LIMIT = 60 * 1024 * 1024


def softplus(value):
    return jnp.maximum(value, 0.0) + jnp.log1p(jnp.exp(-jnp.abs(value)))


def build_kernel(tiles, entries, blocks, row_ref, col_ref, window_ref, near_ref,
                 mats_ref, degree_ref, dst_ref, src_ref, count_ref, stage, sems):
    root = 1.0 / math.sqrt(window_ref.shape[1])
    degree_ref[...] = jnp.zeros_like(degree_ref)
    count_ref[0] = 0
    count_ref[1] = 0
    places = lax.broadcasted_iota(jnp.int32, (BLK, BLK), 0).astype(jnp.float32)

    def emit(mat, slot, dst, src):
        sent = count_ref[0]
        place = lax.rem(sent, STAGE)

        @pl.when(sent >= STAGE)
        def _():
            pltpu.make_async_copy(stage.at[place], mats_ref.at[0], sems.at[place]).wait()

        high = mat.astype(jnp.bfloat16)
        stage[place, :, 0:BLK] = high
        stage[place, :, BLK:] = (mat - high.astype(jnp.float32)).astype(jnp.bfloat16)
        pltpu.make_async_copy(stage.at[place], mats_ref.at[slot], sems.at[place]).start()
        count_ref[0] = sent + 1
        dst_ref[slot] = dst
        src_ref[slot] = src
        rows = pl.ds(pl.multiple_of(dst * BLK, BLK), BLK)
        degree_ref[rows, :] += jnp.broadcast_to(jnp.sum(mat, axis=1, keepdims=True), (BLK, BLK))

    def turned(t):
        left = window_ref[pl.ds(pl.multiple_of(row_ref[t] * BLK, BLK), BLK), :]
        right = window_ref[pl.ds(pl.multiple_of(col_ref[t] * BLK, BLK), BLK), :]
        dots = lax.dot_general(right, left, (((1,), (1,)), ((), ())),
                               preferred_element_type=jnp.float32)
        near = near_ref[t].astype(jnp.float32)
        counted = jnp.zeros((BLK, BLK), jnp.float32)
        for k in range(entries):
            counted += jnp.where(places == near[k:k + 1, :], 1.0, 0.0)
        return counted * softplus(dots * root)

    def mine(t):
        col = col_ref[t]
        return jnp.logical_and(col >= blocks, col < 2 * blocks)

    def emit_back(t, mat):
        slot = tiles + count_ref[1]
        emit(mat, slot, col_ref[t] - blocks, row_ref[t])
        count_ref[1] = slot - tiles + 1

    @pl.loop(0, tiles)
    def _(t):
        mat = turned(t)
        emit(mat.T, t, row_ref[t] - blocks, col_ref[t])

        @pl.when(mine(t))
        def _():
            emit_back(t, mat)

    @pl.loop(tiles, 3 * tiles)
    def _(t):
        @pl.when(mine(t))
        def _():
            emit_back(t, turned(t))

    for place in range(STAGE):
        pltpu.make_async_copy(stage.at[place], mats_ref.at[0], sems.at[place]).wait()


def build(entries, row, col, window, near):
    total = near.shape[0]
    tiles = total // 3
    blocks = window.shape[0] // (3 * BLK)
    smem = pl.BlockSpec(memory_space=pltpu.SMEM)
    vmem = pl.BlockSpec(memory_space=pltpu.VMEM)
    return pl.pallas_call(
        functools.partial(build_kernel, tiles, entries, blocks),
        out_shape=(
            jax.ShapeDtypeStruct((4 * tiles, BLK, 2 * BLK), jnp.bfloat16),
            jax.ShapeDtypeStruct((blocks * BLK, BLK), jnp.float32),
            jax.ShapeDtypeStruct((4 * tiles,), jnp.int32),
            jax.ShapeDtypeStruct((4 * tiles,), jnp.int32),
            jax.ShapeDtypeStruct((2,), jnp.int32),
        ),
        in_specs=[smem, smem, vmem, vmem],
        out_specs=(pl.BlockSpec(memory_space=pl.ANY), vmem, smem, smem, smem),
        scratch_shapes=[
            pltpu.VMEM((STAGE, BLK, 2 * BLK), jnp.bfloat16),
            pltpu.SemaphoreType.DMA((STAGE,)),
        ],
        compiler_params=pltpu.CompilerParams(vmem_limit_bytes=VMEM_LIMIT),
        name="build_tiles",
    )(row, col, window, near)


def step_kernel(step, blocks, tiles, *refs):
    refs = list(refs)

    def take(count):
        taken = refs[:count]
        del refs[:count]
        return taken

    dst_ref, src_ref, count_ref, mats_ref, scale_ref = take(5)
    if step == 0:
        dir_in, halo_in = take(2)
        res_in = dir_in
    else:
        sums_in, res_in, dir_in, image_in = take(4)
        if step == 1:
            (halo_in,) = take(1)
            tail_in = halo_in
        else:
            halo_in, tail_in = take(2)
        fresh_low, fresh_high = take(2)
    if step > 0:
        res_out, dir_out = take(2)
    image_out, sums_out = take(2)
    if step < 2:
        (send_out,) = take(1)
    if step == 1:
        halo_out, tail_out = take(2)
    mats, field, total, sems = refs

    chunks = mats.shape[0] // CHUNK
    used = tiles + count_ref[1]

    def fetch(c):
        span = pl.ds(c * CHUNK, CHUNK)
        return pltpu.make_async_copy(mats_ref.at[span], mats.at[span], sems.at[c])

    for c in range(chunks):
        @pl.when(c * CHUNK < used)
        def _():
            fetch(c).start()

    total[...] = jnp.zeros_like(total)
    sums_out[...] = jnp.zeros_like(sums_out)
    if step > 0:
        norm = sums_in[0:1, :]
        alpha = norm / sums_in[1:2, :]
        after = norm - 2.0 * alpha * sums_in[2:3, :] + alpha * alpha * sums_in[3:4, :]
        beta = after / norm

    def put(block, value):
        high = value.astype(jnp.bfloat16)
        low = (value - high.astype(jnp.float32)).astype(jnp.bfloat16)
        field[block, 0:BLK, 0:BLK] = high
        field[block, 0:BLK, BLK:] = low
        field[block, BLK:, 0:BLK] = high
        field[block, BLK:, BLK:] = low

    def rows_of(b):
        return pl.ds(pl.multiple_of(b * BLK, BLK), BLK)

    @pl.loop(0, blocks)
    def _(b):
        rows = rows_of(b)
        direction = dir_in[rows, :]
        if step > 0:
            residual = res_in[rows, :] - alpha * image_in[rows, :]
            direction = residual + beta * direction
            res_out[rows, :] = residual
            dir_out[rows, :] = direction
        put(blocks + b, direction * scale_ref[rows, :])
        for half in range(2):
            here = rows_of(half * blocks + b)
            value = halo_in[here, :]
            if step > 0:
                fresh = (fresh_low, fresh_high)[half][rows, :]
                tail = tail_in[here, :] - alpha * fresh
                value = tail + beta * value
                if step == 1:
                    halo_out[here, :] = value
                    tail_out[here, :] = tail
            put(2 * half * blocks + b, value)

    def partial(n):
        both = jnp.dot(mats[n], field[src_ref[n]], preferred_element_type=jnp.float32)
        return both[:, 0:BLK] + both[:, BLK:]

    def run(first, count):
        terms = [partial(first + i) for i in range(count)]
        for i in range(count):
            total[rows_of(dst_ref[first + i]), :] += terms[i]

    @pl.loop(0, pl.cdiv(used, CHUNK))
    def _(c):
        fetch(c).wait()
        first = c * CHUNK
        have = jnp.minimum(CHUNK, used - first)

        @pl.loop(0, have // 4)
        def _(g):
            run(first + 4 * g, 4)

        @pl.loop(have // 4 * 4, have)
        def _(i):
            run(first + i, 1)

    @pl.loop(0, blocks)
    def _(b):
        rows = rows_of(b)
        scale = scale_ref[rows, :]
        direction = (dir_out if step > 0 else dir_in)[rows, :]
        residual = (res_out if step > 0 else res_in)[rows, :]
        image = direction - DAMPING * scale * total[rows, :]
        image_out[rows, :] = image
        if step < 2:
            send_out[rows, :] = scale * image
        for place, value in enumerate(
            (residual * residual, direction * image, residual * image, image * image)
        ):
            sums_out[place:place + 1, :] += jnp.sum(value, axis=0, keepdims=True)


def run_step(step, dst, src, count, mats, scale, *rest):
    rows, columns = scale.shape[0], rest[-1].shape[1]
    tiles = dst.shape[0] // 4
    blocks = rows // BLK
    smem = pl.BlockSpec(memory_space=pltpu.SMEM)
    vmem = pl.BlockSpec(memory_space=pltpu.VMEM)
    own = jax.ShapeDtypeStruct((rows, columns), jnp.float32)
    twice = jax.ShapeDtypeStruct((2 * rows, columns), jnp.float32)
    sums = jax.ShapeDtypeStruct((8, columns), jnp.float32)
    outs = ([own, own] if step > 0 else []) + [own, sums]
    if step < 2:
        outs += [own]
    if step == 1:
        outs += [twice, twice]
    return pl.pallas_call(
        functools.partial(step_kernel, step, blocks, tiles),
        out_shape=tuple(outs),
        in_specs=[smem, smem, smem, pl.BlockSpec(memory_space=pl.ANY), vmem]
        + [vmem] * len(rest),
        out_specs=tuple(vmem for _ in outs),
        scratch_shapes=[
            pltpu.VMEM(mats.shape, jnp.bfloat16),
            pltpu.VMEM((3 * blocks, 2 * BLK, 2 * BLK), jnp.bfloat16),
            pltpu.VMEM((rows, columns), jnp.float32),
            pltpu.SemaphoreType.DMA((mats.shape[0] // CHUNK,)),
        ],
        compiler_params=pltpu.CompilerParams(vmem_limit_bytes=VMEM_LIMIT),
        name="operator_step",
    )(dst, src, count, mats, scale, *rest)


def peer(axis, index):
    return {axis: index}


def signal_all(others):
    barrier = pltpu.get_barrier_semaphore()
    for exists, axis, index in others:
        def hello(axis=axis, index=index):
            pl.semaphore_signal(barrier, inc=1, device_id=peer(axis, index),
                                device_id_type=pl.DeviceIdType.MESH)

        if exists is None:
            hello()
        else:
            pl.when(exists)(hello)
    always = sum(exists is None for exists, _, _ in others)
    perhaps = [exists.astype(jnp.int32) for exists, _, _ in others if exists is not None]
    pl.semaphore_wait(barrier, functools.reduce(lambda x, y: x + y, perhaps, always))


def remote(src, dst, send, recv, axis, index):
    return pltpu.make_async_remote_copy(
        src_ref=src, dst_ref=dst, send_sem=send, recv_sem=recv,
        device_id=peer(axis, index), device_id_type=pl.DeviceIdType.MESH,
    )


def sides_of(count):
    me = lax.axis_index("gal")
    up = lax.rem(me + 1, count)
    down = lax.rem(me + count - 1, count)
    return me, ((me + 1 < count, up), (me > 0, down))


def swap_kernel(count, with_field, with_sums, *refs):
    refs = list(refs)
    field = refs.pop(0) if with_field else None
    sums = refs.pop(0) if with_sums else None
    outs = (refs.pop(0), refs.pop(0)) if with_field else None
    sums_out = refs.pop(0) if with_sums else None
    me, sides = sides_of(count)
    if with_sums:
        slots, sum_send, sum_recv = refs[:3]
        refs = refs[3:]
        signal_all([(None, "gal", lax.rem(me + o, count)) for o in range(1, count)])
    else:
        signal_all([(exists, "gal", index) for exists, index in sides])
    if with_sums:
        sends = [
            remote(sums, slots.at[o], sum_send.at[o], sum_recv.at[o], "gal", lax.rem(me + o, count))
            for o in range(1, count)
        ]
        for copy in sends:
            copy.start()
    if with_field:
        send, recv = refs
        copies = [
            remote(field, outs[i], send.at[i], recv.at[i], "gal", index)
            for i, (_, index) in enumerate(sides)
        ]
        for copy, (exists, _) in zip(copies, sides):
            pl.when(exists)(copy.start)
    if with_sums:
        for copy in sends:
            copy.wait()
        all_sums = sums[...]
        for o in range(1, count):
            all_sums += slots[o]
        sums_out[...] = all_sums
    if with_field:
        for i in range(2):
            pl.when(sides[i][0])(copies[i].wait_send)
            pl.when(sides[1 - i][0])(copies[i].wait_recv)


def swap(ident, field=None, sums=None):
    count = lax.axis_size("gal")
    anywhere = pl.BlockSpec(memory_space=pl.ANY)
    vmem = pl.BlockSpec(memory_space=pltpu.VMEM)
    args, specs, outs, out_specs, scratch = [], [], [], [], []
    if field is not None:
        args.append(field)
        specs.append(anywhere)
        outs += [jax.ShapeDtypeStruct(field.shape, field.dtype)] * 2
        out_specs += [anywhere] * 2
    if sums is not None:
        args.append(sums)
        specs.append(vmem)
        outs.append(jax.ShapeDtypeStruct(sums.shape, sums.dtype))
        out_specs.append(vmem)
        scratch += [
            pltpu.VMEM((count,) + sums.shape, sums.dtype),
            pltpu.SemaphoreType.DMA((count,)),
            pltpu.SemaphoreType.DMA((count,)),
        ]
    if field is not None:
        scratch += [pltpu.SemaphoreType.DMA((2,)), pltpu.SemaphoreType.DMA((2,))]
    return pl.pallas_call(
        functools.partial(swap_kernel, count, field is not None, sums is not None),
        out_shape=tuple(outs),
        in_specs=specs,
        out_specs=tuple(out_specs),
        scratch_shapes=scratch,
        compiler_params=pltpu.CompilerParams(collective_id=ident, has_side_effects=True),
        name="swap",
    )(*args)


PIECES = 2


def gather_kernel(count, parts, own, near, window, near_all,
                  far_send, far_recv, local_sems, *level_sems):
    rows, tiles = own.shape[0], near.shape[0]
    size, tile_size = rows // parts, tiles // parts
    step, tile_step = size // PIECES, tile_size // PIECES
    part = lax.axis_index("qry")
    me, sides = sides_of(count)
    bits = [1 << b for b in reversed(range(parts.bit_length() - 1))]

    def partner(bit):
        return part + bit - 2 * bit * lax.rem(part // bit, 2)

    signal_all([(exists, "gal", index) for exists, index in sides]
               + [(None, "qry", partner(bit)) for bit in bits])
    locals_ = [
        pltpu.make_async_copy(own, window.at[pl.ds(rows, rows)], local_sems.at[0]),
        pltpu.make_async_copy(near, near_all.at[pl.ds(0, tiles)], local_sems.at[1]),
    ]

    def pair(index, piece, side):
        at = index * size + piece * step
        near_at = index * tile_size + piece * tile_step
        base = (0, 2 * rows)[side]
        near_base = (tiles, 2 * tiles)[side]
        return (
            (own.at[pl.ds(at, step)], window.at[pl.ds(base + at, step)]),
            (near.at[pl.ds(near_at, tile_step)], near_all.at[pl.ds(near_base + near_at, tile_step)]),
        )

    far = {}
    for piece in range(PIECES):
        for i, (_, index) in enumerate(sides):
            far[piece, i] = [
                remote(src, dst, far_send.at[piece, i, k], far_recv.at[piece, i, k], "gal", index)
                for k, (src, dst) in enumerate(pair(part, piece, i))
            ]
    for piece in range(PIECES):
        for i, (exists, _) in enumerate(sides):
            for copy in far[piece, i]:
                pl.when(exists)(copy.start)
    for copy in locals_:
        copy.start()

    def forward(piece, side, level):
        bit = bits[level]
        held = [part]
        for earlier in bits[:level]:
            held = held + [index + (partner(earlier) - part) for index in held]
        send, recv = level_sems[2 * level:2 * level + 2]
        return [
            remote(spot, spot, send.at[piece, side, n, k], recv.at[piece, side, n, k],
                   "qry", partner(bit))
            for n, index in enumerate(held)
            for k, (_, spot) in enumerate(pair(index, piece, side))
        ]

    order = [(piece, side) for piece in range(PIECES) for side in range(2)]
    for piece, side in order:
        @pl.when(sides[1 - side][0])
        def _(piece=piece, side=side):
            for copy in far[piece, side]:
                copy.wait_recv()
            for copy in forward(piece, side, 0):
                copy.start()

    for level in range(1, len(bits)):
        for piece, side in order:
            @pl.when(sides[1 - side][0])
            def _(piece=piece, side=side, level=level):
                for copy in forward(piece, side, level - 1):
                    copy.wait_recv()
                for copy in forward(piece, side, level):
                    copy.start()

    for piece, side in order:
        @pl.when(sides[1 - side][0])
        def _(piece=piece, side=side):
            for copy in forward(piece, side, len(bits) - 1):
                copy.wait_recv()
            for level in range(len(bits)):
                for copy in forward(piece, side, level):
                    copy.wait_send()

        @pl.when(sides[side][0])
        def _(piece=piece, side=side):
            for copy in far[piece, side]:
                copy.wait_send()

    for copy in locals_:
        copy.wait()


def gather(own, near):
    count, parts = lax.axis_size("gal"), lax.axis_size("qry")
    anywhere = pl.BlockSpec(memory_space=pl.ANY)
    levels = []
    for level in range(parts.bit_length() - 1):
        levels += [pltpu.SemaphoreType.DMA((PIECES, 2, 1 << level, 2))] * 2
    return pl.pallas_call(
        functools.partial(gather_kernel, count, parts),
        out_shape=(
            jax.ShapeDtypeStruct((3 * own.shape[0],) + own.shape[1:], own.dtype),
            jax.ShapeDtypeStruct((3 * near.shape[0],) + near.shape[1:], near.dtype),
        ),
        in_specs=[anywhere] * 2,
        out_specs=(anywhere, anywhere),
        scratch_shapes=[
            pltpu.SemaphoreType.DMA((PIECES, 2, 2)),
            pltpu.SemaphoreType.DMA((PIECES, 2, 2)),
            pltpu.SemaphoreType.DMA((2,)),
        ] + levels,
        compiler_params=pltpu.CompilerParams(collective_id=0, has_side_effects=True),
        name="gather_beside",
    )(own, near)


def per_device(descriptors, query_descriptors, tile_blocks, neighbours):
    rows, width = descriptors.shape
    tiles = tile_blocks.shape[0]
    blocks = rows // BLK
    place = lax.axis_index("gal")
    count = lax.axis_size("gal")
    entries = neighbours.shape[1]

    first = place * blocks
    spot = tile_blocks - jnp.stack([first, first - blocks])[None, :]
    spots = jnp.pad(spot, ((0, 0), (0, BLK - 2)))[:, None, :]
    near = jnp.concatenate([neighbours, spots], axis=1)
    near = jnp.pad(near, ((0, 0), (0, 16 - entries - 1), (0, 0))).astype(jnp.bfloat16)
    window, near_all = gather(descriptors, near)
    spots = near_all[:, entries, 0:2].astype(jnp.int32)
    shift = jnp.repeat(jnp.array([0, -1, 1], jnp.int32), tiles)
    origin = shift + place
    exists = jnp.logical_and(origin >= 0, origin < count)
    row = spots[:, 0] + (1 + shift) * blocks
    col = jnp.where(exists, spots[:, 1] + shift * blocks, jnp.int32(3 * blocks))

    mats, degree, dst, src, used = build(entries, row, col, window, near_all)
    scale = 1.0 / jnp.sqrt(1.0 + degree)
    scale_low, scale_high = swap(1, scale[:, 0].reshape(blocks, BLK))
    seeds = jax.nn.softplus(
        lax.dot_general(window, query_descriptors, (((1,), (1,)), ((), ())),
                        preferred_element_type=jnp.float32) / math.sqrt(width)
    )
    own = seeds[rows:2 * rows]
    halo = jnp.concatenate(
        [seeds[:rows] * scale_low.reshape(rows, 1), seeds[2 * rows:] * scale_high.reshape(rows, 1)],
        axis=0,
    )
    image0, sums0, send0 = run_step(0, dst, src, used, mats, scale, own, halo)
    low0, high0, sums0 = swap(2, send0, sums0)
    res1, dir1, image1, sums1, send1, halo1, tail1 = run_step(
        1, dst, src, used, mats, scale, sums0, own, own, image0, halo, low0, high0
    )
    low1, high1, sums1 = swap(2, send1, sums1)
    res2, dir2, image2, sums2 = run_step(
        2, dst, src, used, mats, scale, sums1, res1, dir1, image1, halo1, tail1, low1, high1
    )
    (sums2,) = swap(3, None, sums2)
    alpha0, alpha1, alpha2 = (s[0:1] / s[1:2] for s in (sums0, sums1, sums2))
    ranking = alpha0 * own + alpha1 * dir1 + alpha2 * dir2
    residual = res2 - alpha2 * image2
    return ranking, residual


def solution(mesh):
    placed = (P("gal", None), P("qry", None), P("gal", None), P("gal", None, None))
    return jax.shard_map(
        per_device,
        mesh=mesh,
        in_specs=placed,
        out_specs=(P("gal", "qry"), P("gal", "qry")),
        check_vma=False,
    )
```

```python
import functools
import math

import jax
import jax.numpy as jnp
from jax import lax
from jax.experimental import pallas as pl
from jax.experimental.pallas import tpu as pltpu
from jax.sharding import PartitionSpec as P

BLK = 128
DAMPING = 0.99
STAGE = 8
GROUP = 2
CHUNK = 16
VMEM_LIMIT = 60 * 1024 * 1024


def softplus(value):
    return jnp.maximum(value, 0.0) + jnp.log(1.0 + jnp.exp(-jnp.abs(value)))


def build_kernel(tiles, entries, blocks, row_ref, col_ref, window_ref, near_ref,
                 mats_ref, degree_ref, dst_ref, src_ref, count_ref, stage, listed, sems):
    root = 1.0 / math.sqrt(window_ref.shape[1])
    degree_ref[...] = jnp.zeros_like(degree_ref)
    count_ref[0] = 0
    count_ref[1] = 0
    places = lax.broadcasted_iota(jnp.int32, (BLK, BLK), 0).astype(jnp.float32).astype(jnp.bfloat16)
    ones = jnp.ones((2 * BLK, BLK), jnp.bfloat16)
    one, none = jnp.bfloat16(1.0), jnp.bfloat16(0.0)

    def emit(mat, slot, dst, src):
        sent = count_ref[0]
        place = lax.rem(sent, STAGE)

        @pl.when(sent >= STAGE)
        def _():
            pltpu.make_async_copy(stage.at[place], mats_ref.at[0], sems.at[place]).wait()

        high = mat.astype(jnp.bfloat16)
        both = jnp.concatenate([high, (mat - high.astype(jnp.float32)).astype(jnp.bfloat16)], axis=1)
        stage[place] = both
        pltpu.make_async_copy(stage.at[place], mats_ref.at[slot], sems.at[place]).start()
        count_ref[0] = sent + 1
        dst_ref[slot] = dst
        src_ref[slot] = src
        rows = pl.ds(pl.multiple_of(dst * BLK, BLK), BLK)
        degree_ref[rows, :] += jnp.dot(both, ones, preferred_element_type=jnp.float32)

    def turned(t):
        left = window_ref[pl.ds(pl.multiple_of(row_ref[t] * BLK, BLK), BLK), :]
        right = window_ref[pl.ds(pl.multiple_of(col_ref[t] * BLK, BLK), BLK), :]
        dots = lax.dot_general(right, left, (((1,), (1,)), ((), ())),
                               preferred_element_type=jnp.float32)
        near = near_ref[t]
        counted = jnp.zeros((BLK, BLK), jnp.bfloat16)
        for k in range(entries):
            counted += jnp.where(places == near[k:k + 1, :], one, none)
        return counted.astype(jnp.float32) * softplus(dots * root)

    def mine(t):
        col = col_ref[t]
        return jnp.logical_and(col >= blocks, col < 2 * blocks)

    def emit_back(t, mat):
        slot = tiles + count_ref[1]
        emit(mat, slot, col_ref[t] - blocks, row_ref[t])
        count_ref[1] = slot - tiles + 1

    listed[0] = tiles

    def note(t, found):
        @pl.when(mine(t))
        def _():
            listed[found] = t

        return found + mine(t).astype(jnp.int32)

    found = lax.fori_loop(tiles, 3 * tiles, note, jnp.int32(0))

    @pl.loop(0, tiles // GROUP)
    def _(g):
        ids = [g * GROUP + i for i in range(GROUP)]
        mats = [turned(t) for t in ids]
        for t, mat in zip(ids, mats):
            emit(mat.T, t, row_ref[t] - blocks, col_ref[t])
        for t, mat in zip(ids, mats):
            @pl.when(mine(t))
            def _(t=t, mat=mat):
                emit_back(t, mat)

    @pl.loop(0, pl.cdiv(found, GROUP))
    def _(g):
        at = [g * GROUP + i for i in range(GROUP)]
        ids = [listed[jnp.minimum(n, found - 1)] for n in at]
        mats = [turned(t) for t in ids]
        for n, t, mat in zip(at, ids, mats):
            @pl.when(n < found)
            def _(t=t, mat=mat):
                emit_back(t, mat)

    for place in range(STAGE):
        pltpu.make_async_copy(stage.at[place], mats_ref.at[0], sems.at[place]).wait()


def build(entries, row, col, window, near):
    total = near.shape[0]
    tiles = total // 3
    blocks = window.shape[0] // (3 * BLK)
    smem = pl.BlockSpec(memory_space=pltpu.SMEM)
    vmem = pl.BlockSpec(memory_space=pltpu.VMEM)
    return pl.pallas_call(
        functools.partial(build_kernel, tiles, entries, blocks),
        out_shape=(
            jax.ShapeDtypeStruct((4 * tiles, BLK, 2 * BLK), jnp.bfloat16),
            jax.ShapeDtypeStruct((blocks * BLK, BLK), jnp.float32),
            jax.ShapeDtypeStruct((4 * tiles,), jnp.int32),
            jax.ShapeDtypeStruct((4 * tiles,), jnp.int32),
            jax.ShapeDtypeStruct((2,), jnp.int32),
        ),
        in_specs=[smem, smem, vmem, vmem],
        out_specs=(pl.BlockSpec(memory_space=pl.ANY), vmem, smem, smem, smem),
        scratch_shapes=[
            pltpu.VMEM((STAGE, BLK, 2 * BLK), jnp.bfloat16),
            pltpu.SMEM((2 * tiles,), jnp.int32),
            pltpu.SemaphoreType.DMA((STAGE,)),
        ],
        compiler_params=pltpu.CompilerParams(vmem_limit_bytes=VMEM_LIMIT),
        name="build_tiles",
    )(row, col, window, near)


def step_kernel(step, blocks, tiles, *refs):
    refs = list(refs)

    def take(count):
        taken = refs[:count]
        del refs[:count]
        return taken

    dst_ref, src_ref, count_ref, mats_ref, scale_ref = take(5)
    if step == 0:
        dir_in, halo_in = take(2)
        res_in = dir_in
    else:
        sums_in, res_in, dir_in, image_in = take(4)
        if step == 1:
            (halo_in,) = take(1)
            tail_in = halo_in
        else:
            halo_in, tail_in = take(2)
        fresh_low, fresh_high = take(2)
    if step > 0:
        res_out, dir_out = take(2)
    image_out, sums_out = take(2)
    if step < 2:
        (send_out,) = take(1)
    if step == 1:
        halo_out, tail_out = take(2)
    mats, field, total, sems = refs

    chunks = mats.shape[0] // CHUNK
    used = tiles + count_ref[1]

    def fetch(c):
        span = pl.ds(c * CHUNK, CHUNK)
        return pltpu.make_async_copy(mats_ref.at[span], mats.at[span], sems.at[c])

    for c in range(chunks):
        @pl.when(c * CHUNK < used)
        def _():
            fetch(c).start()

    total[...] = jnp.zeros_like(total)
    sums_out[...] = jnp.zeros_like(sums_out)
    if step > 0:
        norm = sums_in[0:1, :]
        alpha = norm / sums_in[1:2, :]
        after = norm - 2.0 * alpha * sums_in[2:3, :] + alpha * alpha * sums_in[3:4, :]
        beta = after / norm

    def put(block, value):
        high = value.astype(jnp.bfloat16)
        low = (value - high.astype(jnp.float32)).astype(jnp.bfloat16)
        field[block, 0:BLK, 0:BLK] = high
        field[block, 0:BLK, BLK:] = low
        field[block, BLK:, 0:BLK] = high
        field[block, BLK:, BLK:] = low

    def rows_of(b):
        return pl.ds(pl.multiple_of(b * BLK, BLK), BLK)

    @pl.loop(0, blocks)
    def _(b):
        rows = rows_of(b)
        direction = dir_in[rows, :]
        if step > 0:
            residual = res_in[rows, :] - alpha * image_in[rows, :]
            direction = residual + beta * direction
            res_out[rows, :] = residual
            dir_out[rows, :] = direction
        put(blocks + b, direction * scale_ref[rows, :])
        for half in range(2):
            here = rows_of(half * blocks + b)
            value = halo_in[here, :]
            if step > 0:
                fresh = (fresh_low, fresh_high)[half][rows, :]
                tail = tail_in[here, :] - alpha * fresh
                value = tail + beta * value
                if step == 1:
                    halo_out[here, :] = value
                    tail_out[here, :] = tail
            put(2 * half * blocks + b, value)

    def partial(n):
        both = jnp.dot(mats[n], field[src_ref[n]], preferred_element_type=jnp.float32)
        return both[:, 0:BLK] + both[:, BLK:]

    def run(first, count):
        terms = [partial(first + i) for i in range(count)]
        for i in range(count):
            total[rows_of(dst_ref[first + i]), :] += terms[i]

    @pl.loop(0, pl.cdiv(used, CHUNK))
    def _(c):
        fetch(c).wait()
        first = c * CHUNK
        have = jnp.minimum(CHUNK, used - first)

        @pl.loop(0, have // 4)
        def _(g):
            run(first + 4 * g, 4)

        @pl.loop(have // 4 * 4, have)
        def _(i):
            run(first + i, 1)

    @pl.loop(0, blocks)
    def _(b):
        rows = rows_of(b)
        scale = scale_ref[rows, :]
        direction = (dir_out if step > 0 else dir_in)[rows, :]
        residual = (res_out if step > 0 else res_in)[rows, :]
        image = direction - DAMPING * scale * total[rows, :]
        image_out[rows, :] = image
        if step < 2:
            send_out[rows, :] = scale * image
        for place, value in enumerate(
            (residual * residual, direction * image, residual * image, image * image)
        ):
            sums_out[place:place + 1, :] += jnp.sum(value, axis=0, keepdims=True)


def run_step(step, dst, src, count, mats, scale, *rest):
    rows, columns = scale.shape[0], rest[-1].shape[1]
    tiles = dst.shape[0] // 4
    blocks = rows // BLK
    smem = pl.BlockSpec(memory_space=pltpu.SMEM)
    vmem = pl.BlockSpec(memory_space=pltpu.VMEM)
    own = jax.ShapeDtypeStruct((rows, columns), jnp.float32)
    twice = jax.ShapeDtypeStruct((2 * rows, columns), jnp.float32)
    sums = jax.ShapeDtypeStruct((8, columns), jnp.float32)
    outs = ([own, own] if step > 0 else []) + [own, sums]
    if step < 2:
        outs += [own]
    if step == 1:
        outs += [twice, twice]
    return pl.pallas_call(
        functools.partial(step_kernel, step, blocks, tiles),
        out_shape=tuple(outs),
        in_specs=[smem, smem, smem, pl.BlockSpec(memory_space=pl.ANY), vmem]
        + [vmem] * len(rest),
        out_specs=tuple(vmem for _ in outs),
        scratch_shapes=[
            pltpu.VMEM(mats.shape, jnp.bfloat16),
            pltpu.VMEM((3 * blocks, 2 * BLK, 2 * BLK), jnp.bfloat16),
            pltpu.VMEM((rows, columns), jnp.float32),
            pltpu.SemaphoreType.DMA((mats.shape[0] // CHUNK,)),
        ],
        compiler_params=pltpu.CompilerParams(vmem_limit_bytes=VMEM_LIMIT),
        name="operator_step",
    )(dst, src, count, mats, scale, *rest)


def peer(axis, index):
    return {axis: index}


def signal_all(others):
    barrier = pltpu.get_barrier_semaphore()
    for exists, axis, index in others:
        def hello(axis=axis, index=index):
            pl.semaphore_signal(barrier, inc=1, device_id=peer(axis, index),
                                device_id_type=pl.DeviceIdType.MESH)

        if exists is None:
            hello()
        else:
            pl.when(exists)(hello)
    always = sum(exists is None for exists, _, _ in others)
    perhaps = [exists.astype(jnp.int32) for exists, _, _ in others if exists is not None]
    pl.semaphore_wait(barrier, functools.reduce(lambda x, y: x + y, perhaps, always))


def remote(src, dst, send, recv, axis, index):
    return pltpu.make_async_remote_copy(
        src_ref=src, dst_ref=dst, send_sem=send, recv_sem=recv,
        device_id=peer(axis, index), device_id_type=pl.DeviceIdType.MESH,
    )


def sides_of(count):
    me = lax.axis_index("gal")
    up = lax.rem(me + 1, count)
    down = lax.rem(me + count - 1, count)
    return me, ((me + 1 < count, up), (me > 0, down))


def swap_kernel(count, with_field, with_sums, *refs):
    refs = list(refs)
    field = refs.pop(0) if with_field else None
    sums = refs.pop(0) if with_sums else None
    outs = (refs.pop(0), refs.pop(0)) if with_field else None
    sums_out = refs.pop(0) if with_sums else None
    me, sides = sides_of(count)
    if with_sums:
        slots, sum_send, sum_recv = refs[:3]
        refs = refs[3:]
        signal_all([(None, "gal", lax.rem(me + o, count)) for o in range(1, count)])
    else:
        signal_all([(exists, "gal", index) for exists, index in sides])
    if with_sums:
        sends = [
            remote(sums, slots.at[o], sum_send.at[o], sum_recv.at[o], "gal", lax.rem(me + o, count))
            for o in range(1, count)
        ]
        for copy in sends:
            copy.start()
    if with_field:
        send, recv = refs
        copies = [
            remote(field, outs[i], send.at[i], recv.at[i], "gal", index)
            for i, (_, index) in enumerate(sides)
        ]
        for copy, (exists, _) in zip(copies, sides):
            pl.when(exists)(copy.start)
    if with_sums:
        for copy in sends:
            copy.wait()
        all_sums = sums[...]
        for o in range(1, count):
            all_sums += slots[o]
        sums_out[...] = all_sums
    if with_field:
        for i in range(2):
            pl.when(sides[i][0])(copies[i].wait_send)
            pl.when(sides[1 - i][0])(copies[i].wait_recv)


def swap(ident, field=None, sums=None):
    count = lax.axis_size("gal")
    anywhere = pl.BlockSpec(memory_space=pl.ANY)
    vmem = pl.BlockSpec(memory_space=pltpu.VMEM)
    args, specs, outs, out_specs, scratch = [], [], [], [], []
    if field is not None:
        args.append(field)
        specs.append(anywhere)
        outs += [jax.ShapeDtypeStruct(field.shape, field.dtype)] * 2
        out_specs += [anywhere] * 2
    if sums is not None:
        args.append(sums)
        specs.append(vmem)
        outs.append(jax.ShapeDtypeStruct(sums.shape, sums.dtype))
        out_specs.append(vmem)
        scratch += [
            pltpu.VMEM((count,) + sums.shape, sums.dtype),
            pltpu.SemaphoreType.DMA((count,)),
            pltpu.SemaphoreType.DMA((count,)),
        ]
    if field is not None:
        scratch += [pltpu.SemaphoreType.DMA((2,)), pltpu.SemaphoreType.DMA((2,))]
    return pl.pallas_call(
        functools.partial(swap_kernel, count, field is not None, sums is not None),
        out_shape=tuple(outs),
        in_specs=specs,
        out_specs=tuple(out_specs),
        scratch_shapes=scratch,
        compiler_params=pltpu.CompilerParams(collective_id=ident, has_side_effects=True),
        name="swap",
    )(*args)


PIECES = 4


def gather_kernel(count, parts, own, near, window, near_all,
                  far_send, far_recv, local_sems, *level_sems):
    rows, tiles = own.shape[0], near.shape[0]
    size, tile_size = rows // parts, tiles // parts
    step, tile_step = size // PIECES, tile_size // PIECES
    part = lax.axis_index("qry")
    me, sides = sides_of(count)
    bits = [1 << b for b in reversed(range(parts.bit_length() - 1))]

    def partner(bit):
        return part + bit - 2 * bit * lax.rem(part // bit, 2)

    signal_all([(exists, "gal", index) for exists, index in sides]
               + [(None, "qry", partner(bit)) for bit in bits])
    locals_ = [
        pltpu.make_async_copy(own, window.at[pl.ds(rows, rows)], local_sems.at[0]),
        pltpu.make_async_copy(near, near_all.at[pl.ds(0, tiles)], local_sems.at[1]),
    ]

    def pair(index, piece, side):
        at = index * size + piece * step
        near_at = index * tile_size + piece * tile_step
        base = (0, 2 * rows)[side]
        near_base = (tiles, 2 * tiles)[side]
        return (
            (own.at[pl.ds(at, step)], window.at[pl.ds(base + at, step)]),
            (near.at[pl.ds(near_at, tile_step)], near_all.at[pl.ds(near_base + near_at, tile_step)]),
        )

    far = {}
    for piece in range(PIECES):
        for i, (_, index) in enumerate(sides):
            far[piece, i] = [
                remote(src, dst, far_send.at[piece, i, k], far_recv.at[piece, i, k], "gal", index)
                for k, (src, dst) in enumerate(pair(part, piece, i))
            ]
    for piece in range(PIECES):
        for i, (exists, _) in enumerate(sides):
            for copy in far[piece, i]:
                pl.when(exists)(copy.start)
    for copy in locals_:
        copy.start()

    def forward(piece, side, level):
        bit = bits[level]
        held = [part]
        for earlier in bits[:level]:
            held = held + [index + (partner(earlier) - part) for index in held]
        send, recv = level_sems[2 * level:2 * level + 2]
        return [
            remote(spot, spot, send.at[piece, side, n, k], recv.at[piece, side, n, k],
                   "qry", partner(bit))
            for n, index in enumerate(held)
            for k, (_, spot) in enumerate(pair(index, piece, side))
        ]

    order = [(piece, side) for piece in range(PIECES) for side in range(2)]
    depth = len(bits)
    for turn in range(len(order) + depth - 1):
        for level in range(depth):
            if not 0 <= turn - level < len(order):
                continue
            piece, side = order[turn - level]

            @pl.when(sides[1 - side][0])
            def _(piece=piece, side=side, level=level):
                for copy in forward(piece, side, level - 1) if level else far[piece, side]:
                    copy.wait_recv()
                for copy in forward(piece, side, level):
                    copy.start()

    for piece, side in order:
        @pl.when(sides[1 - side][0])
        def _(piece=piece, side=side):
            for copy in forward(piece, side, len(bits) - 1):
                copy.wait_recv()
            for level in range(len(bits)):
                for copy in forward(piece, side, level):
                    copy.wait_send()

        @pl.when(sides[side][0])
        def _(piece=piece, side=side):
            for copy in far[piece, side]:
                copy.wait_send()

    for copy in locals_:
        copy.wait()


def gather(own, near):
    count, parts = lax.axis_size("gal"), lax.axis_size("qry")
    anywhere = pl.BlockSpec(memory_space=pl.ANY)
    levels = []
    for level in range(parts.bit_length() - 1):
        levels += [pltpu.SemaphoreType.DMA((PIECES, 2, 1 << level, 2))] * 2
    return pl.pallas_call(
        functools.partial(gather_kernel, count, parts),
        out_shape=(
            jax.ShapeDtypeStruct((3 * own.shape[0],) + own.shape[1:], own.dtype),
            jax.ShapeDtypeStruct((3 * near.shape[0],) + near.shape[1:], near.dtype),
        ),
        in_specs=[anywhere] * 2,
        out_specs=(anywhere, anywhere),
        scratch_shapes=[
            pltpu.SemaphoreType.DMA((PIECES, 2, 2)),
            pltpu.SemaphoreType.DMA((PIECES, 2, 2)),
            pltpu.SemaphoreType.DMA((2,)),
        ] + levels,
        compiler_params=pltpu.CompilerParams(collective_id=0, has_side_effects=True),
        name="gather_beside",
    )(own, near)


def per_device(descriptors, query_descriptors, tile_blocks, neighbours):
    rows, width = descriptors.shape
    tiles = tile_blocks.shape[0]
    blocks = rows // BLK
    place = lax.axis_index("gal")
    count = lax.axis_size("gal")
    entries = neighbours.shape[1]

    first = place * blocks
    spot = tile_blocks - jnp.stack([first, first - blocks])[None, :]
    spots = jnp.pad(spot, ((0, 0), (0, BLK - 2)))[:, None, :]
    near = jnp.concatenate([neighbours, spots], axis=1)
    near = jnp.pad(near, ((0, 0), (0, 16 - entries - 1), (0, 0))).astype(jnp.bfloat16)
    window, near_all = gather(descriptors, near)
    spots = near_all[:, entries, 0:2].astype(jnp.int32)
    shift = jnp.repeat(jnp.array([0, -1, 1], jnp.int32), tiles)
    origin = shift + place
    exists = jnp.logical_and(origin >= 0, origin < count)
    row = spots[:, 0] + (1 + shift) * blocks
    col = jnp.where(exists, spots[:, 1] + shift * blocks, jnp.int32(3 * blocks))

    mats, degree, dst, src, used = build(entries, row, col, window, near_all)
    scale = 1.0 / jnp.sqrt(1.0 + degree)
    scale_low, scale_high = swap(1, scale[:, 0].reshape(blocks, BLK))
    seeds = jax.nn.softplus(
        lax.dot_general(window, query_descriptors, (((1,), (1,)), ((), ())),
                        preferred_element_type=jnp.float32) / math.sqrt(width)
    )
    own = seeds[rows:2 * rows]
    halo = jnp.concatenate(
        [seeds[:rows] * scale_low.reshape(rows, 1), seeds[2 * rows:] * scale_high.reshape(rows, 1)],
        axis=0,
    )
    image0, sums0, send0 = run_step(0, dst, src, used, mats, scale, own, halo)
    low0, high0, sums0 = swap(2, send0, sums0)
    res1, dir1, image1, sums1, send1, halo1, tail1 = run_step(
        1, dst, src, used, mats, scale, sums0, own, own, image0, halo, low0, high0
    )
    low1, high1, sums1 = swap(2, send1, sums1)
    res2, dir2, image2, sums2 = run_step(
        2, dst, src, used, mats, scale, sums1, res1, dir1, image1, halo1, tail1, low1, high1
    )
    (sums2,) = swap(3, None, sums2)
    alpha0, alpha1, alpha2 = (s[0:1] / s[1:2] for s in (sums0, sums1, sums2))
    ranking = alpha0 * own + alpha1 * dir1 + alpha2 * dir2
    residual = res2 - alpha2 * image2
    return ranking, residual


def solution(mesh):
    placed = (P("gal", None), P("qry", None), P("gal", None), P("gal", None, None))
    return jax.shard_map(
        per_device,
        mesh=mesh,
        in_specs=placed,
        out_specs=(P("gal", "qry"), P("gal", "qry")),
        check_vma=False,
    )
```

```python
import functools
import math

import jax
import jax.numpy as jnp
from jax import lax
from jax.experimental import pallas as pl
from jax.experimental.pallas import tpu as pltpu
from jax.sharding import PartitionSpec as P

BLK = 128
DAMPING = 0.99
STAGE = 8
GROUP = 2
CHUNK = 16
VMEM_LIMIT = 60 * 1024 * 1024


def softplus(value):
    return jnp.maximum(value, 0.0) + jnp.log(1.0 + jnp.exp(-jnp.abs(value)))


def build_kernel(tiles, entries, blocks, row_ref, col_ref, own_ref, beside_ref, near_own, near_beside,
                 mats_ref, degree_ref, dst_ref, src_ref, count_ref,
                 window_ref, near_ref, stage, listed, load_sems, sems):
    size = blocks * BLK
    loads = [
        pltpu.make_async_copy(src, dst, load_sems.at[i])
        for i, (src, dst) in enumerate((
            (own_ref, window_ref.at[pl.ds(size, size)]),
            (beside_ref.at[pl.ds(0, size)], window_ref.at[pl.ds(0, size)]),
            (beside_ref.at[pl.ds(size, size)], window_ref.at[pl.ds(2 * size, size)]),
            (near_own, near_ref.at[pl.ds(0, tiles)]),
            (near_beside, near_ref.at[pl.ds(tiles, 2 * tiles)]),
        ))
    ]
    for load in loads:
        load.start()
    root = 1.0 / math.sqrt(window_ref.shape[1])
    degree_ref[...] = jnp.zeros_like(degree_ref)
    count_ref[0] = 0
    count_ref[1] = 0
    places = lax.broadcasted_iota(jnp.int32, (BLK, BLK), 0).astype(jnp.float32).astype(jnp.bfloat16)
    ones = jnp.ones((2 * BLK, BLK), jnp.bfloat16)
    one, none = jnp.bfloat16(1.0), jnp.bfloat16(0.0)

    def emit(mat, slot, dst, src):
        sent = count_ref[0]
        place = lax.rem(sent, STAGE)

        @pl.when(sent >= STAGE)
        def _():
            pltpu.make_async_copy(stage.at[place], mats_ref.at[0], sems.at[place]).wait()

        high = mat.astype(jnp.bfloat16)
        both = jnp.concatenate([high, (mat - high.astype(jnp.float32)).astype(jnp.bfloat16)], axis=1)
        stage[place] = both
        pltpu.make_async_copy(stage.at[place], mats_ref.at[slot], sems.at[place]).start()
        count_ref[0] = sent + 1
        dst_ref[slot] = dst
        src_ref[slot] = src
        rows = pl.ds(pl.multiple_of(dst * BLK, BLK), BLK)
        degree_ref[rows, :] += jnp.dot(both, ones, preferred_element_type=jnp.float32)

    def turned(t):
        left = window_ref[pl.ds(pl.multiple_of(row_ref[t] * BLK, BLK), BLK), :]
        right = window_ref[pl.ds(pl.multiple_of(col_ref[t] * BLK, BLK), BLK), :]
        dots = lax.dot_general(right, left, (((1,), (1,)), ((), ())),
                               preferred_element_type=jnp.float32)
        near = near_ref[t]
        counted = jnp.zeros((BLK, BLK), jnp.bfloat16)
        for k in range(entries):
            counted += jnp.where(places == near[k:k + 1, :], one, none)
        return counted.astype(jnp.float32) * softplus(dots * root)

    def mine(t):
        col = col_ref[t]
        return jnp.logical_and(col >= blocks, col < 2 * blocks)

    def emit_back(t, mat):
        slot = tiles + count_ref[1]
        emit(mat, slot, col_ref[t] - blocks, row_ref[t])
        count_ref[1] = slot - tiles + 1

    listed[0] = tiles

    def note(t, found):
        @pl.when(mine(t))
        def _():
            listed[found] = t

        return found + mine(t).astype(jnp.int32)

    found = lax.fori_loop(tiles, 3 * tiles, note, jnp.int32(0))
    for load in loads:
        load.wait()

    @pl.loop(0, tiles // GROUP)
    def _(g):
        ids = [g * GROUP + i for i in range(GROUP)]
        mats = [turned(t) for t in ids]
        for t, mat in zip(ids, mats):
            emit(mat.T, t, row_ref[t] - blocks, col_ref[t])
        for t, mat in zip(ids, mats):
            @pl.when(mine(t))
            def _(t=t, mat=mat):
                emit_back(t, mat)

    @pl.loop(0, pl.cdiv(found, GROUP))
    def _(g):
        at = [g * GROUP + i for i in range(GROUP)]
        ids = [listed[jnp.minimum(n, found - 1)] for n in at]
        mats = [turned(t) for t in ids]
        for n, t, mat in zip(at, ids, mats):
            @pl.when(n < found)
            def _(t=t, mat=mat):
                emit_back(t, mat)

    for place in range(STAGE):
        pltpu.make_async_copy(stage.at[place], mats_ref.at[0], sems.at[place]).wait()


def build(entries, row, col, own, beside, near, near_beside):
    tiles = near.shape[0]
    blocks = own.shape[0] // BLK
    anywhere = pl.BlockSpec(memory_space=pl.ANY)
    smem = pl.BlockSpec(memory_space=pltpu.SMEM)
    vmem = pl.BlockSpec(memory_space=pltpu.VMEM)
    return pl.pallas_call(
        functools.partial(build_kernel, tiles, entries, blocks),
        out_shape=(
            jax.ShapeDtypeStruct((4 * tiles, BLK, 2 * BLK), jnp.bfloat16),
            jax.ShapeDtypeStruct((blocks * BLK, BLK), jnp.float32),
            jax.ShapeDtypeStruct((4 * tiles,), jnp.int32),
            jax.ShapeDtypeStruct((4 * tiles,), jnp.int32),
            jax.ShapeDtypeStruct((2,), jnp.int32),
        ),
        in_specs=[smem, smem] + [anywhere] * 4,
        out_specs=(pl.BlockSpec(memory_space=pl.ANY), vmem, smem, smem, smem),
        scratch_shapes=[
            pltpu.VMEM((3 * own.shape[0],) + own.shape[1:], own.dtype),
            pltpu.VMEM((3 * tiles,) + near.shape[1:], near.dtype),
            pltpu.VMEM((STAGE, BLK, 2 * BLK), jnp.bfloat16),
            pltpu.SMEM((2 * tiles,), jnp.int32),
            pltpu.SemaphoreType.DMA((5,)),
            pltpu.SemaphoreType.DMA((STAGE,)),
        ],
        compiler_params=pltpu.CompilerParams(vmem_limit_bytes=VMEM_LIMIT),
        name="build_tiles",
    )(row, col, own, beside, near, near_beside)


def step_kernel(step, blocks, tiles, *refs):
    refs = list(refs)

    def take(count):
        taken = refs[:count]
        del refs[:count]
        return taken

    dst_ref, src_ref, count_ref, mats_ref, scale_ref = take(5)
    if step == 0:
        dir_in, halo_in = take(2)
        res_in = dir_in
    else:
        sums_in, res_in, dir_in, image_in = take(4)
        if step == 1:
            (halo_in,) = take(1)
            tail_in = halo_in
        else:
            halo_in, tail_in = take(2)
        fresh_low, fresh_high = take(2)
    if step > 0:
        res_out, dir_out = take(2)
    image_out, sums_out = take(2)
    if step < 2:
        (send_out,) = take(1)
    if step == 1:
        halo_out, tail_out = take(2)
    mats, field, total, sems = refs

    chunks = mats.shape[0] // CHUNK
    used = tiles + count_ref[1]

    def fetch(c):
        span = pl.ds(c * CHUNK, CHUNK)
        return pltpu.make_async_copy(mats_ref.at[span], mats.at[span], sems.at[c])

    for c in range(chunks):
        @pl.when(c * CHUNK < used)
        def _():
            fetch(c).start()

    total[...] = jnp.zeros_like(total)
    sums_out[...] = jnp.zeros_like(sums_out)
    if step > 0:
        norm = sums_in[0:1, :]
        alpha = norm / sums_in[1:2, :]
        after = norm - 2.0 * alpha * sums_in[2:3, :] + alpha * alpha * sums_in[3:4, :]
        beta = after / norm

    def put(block, value):
        high = value.astype(jnp.bfloat16)
        low = (value - high.astype(jnp.float32)).astype(jnp.bfloat16)
        field[block, 0:BLK, 0:BLK] = high
        field[block, 0:BLK, BLK:] = low
        field[block, BLK:, 0:BLK] = high
        field[block, BLK:, BLK:] = low

    def rows_of(b):
        return pl.ds(pl.multiple_of(b * BLK, BLK), BLK)

    @pl.loop(0, blocks)
    def _(b):
        rows = rows_of(b)
        direction = dir_in[rows, :]
        if step > 0:
            residual = res_in[rows, :] - alpha * image_in[rows, :]
            direction = residual + beta * direction
            res_out[rows, :] = residual
            dir_out[rows, :] = direction
        put(blocks + b, direction * scale_ref[rows, :])
        for half in range(2):
            here = rows_of(half * blocks + b)
            value = halo_in[here, :]
            if step > 0:
                fresh = (fresh_low, fresh_high)[half][rows, :]
                tail = tail_in[here, :] - alpha * fresh
                value = tail + beta * value
                if step == 1:
                    halo_out[here, :] = value
                    tail_out[here, :] = tail
            put(2 * half * blocks + b, value)

    def partial(n):
        both = jnp.dot(mats[n], field[src_ref[n]], preferred_element_type=jnp.float32)
        return both[:, 0:BLK] + both[:, BLK:]

    def run(first, count):
        terms = [partial(first + i) for i in range(count)]
        for i in range(count):
            total[rows_of(dst_ref[first + i]), :] += terms[i]

    @pl.loop(0, pl.cdiv(used, CHUNK))
    def _(c):
        fetch(c).wait()
        first = c * CHUNK
        have = jnp.minimum(CHUNK, used - first)

        @pl.loop(0, have // 4)
        def _(g):
            run(first + 4 * g, 4)

        @pl.loop(have // 4 * 4, have)
        def _(i):
            run(first + i, 1)

    @pl.loop(0, blocks)
    def _(b):
        rows = rows_of(b)
        scale = scale_ref[rows, :]
        direction = (dir_out if step > 0 else dir_in)[rows, :]
        residual = (res_out if step > 0 else res_in)[rows, :]
        image = direction - DAMPING * scale * total[rows, :]
        image_out[rows, :] = image
        if step < 2:
            send_out[rows, :] = scale * image
        for place, value in enumerate(
            (residual * residual, direction * image, residual * image, image * image)
        ):
            sums_out[place:place + 1, :] += jnp.sum(value, axis=0, keepdims=True)


def run_step(step, dst, src, count, mats, scale, *rest):
    rows, columns = scale.shape[0], rest[-1].shape[1]
    tiles = dst.shape[0] // 4
    blocks = rows // BLK
    smem = pl.BlockSpec(memory_space=pltpu.SMEM)
    vmem = pl.BlockSpec(memory_space=pltpu.VMEM)
    own = jax.ShapeDtypeStruct((rows, columns), jnp.float32)
    twice = jax.ShapeDtypeStruct((2 * rows, columns), jnp.float32)
    sums = jax.ShapeDtypeStruct((8, columns), jnp.float32)
    outs = ([own, own] if step > 0 else []) + [own, sums]
    if step < 2:
        outs += [own]
    if step == 1:
        outs += [twice, twice]
    return pl.pallas_call(
        functools.partial(step_kernel, step, blocks, tiles),
        out_shape=tuple(outs),
        in_specs=[smem, smem, smem, pl.BlockSpec(memory_space=pl.ANY), vmem]
        + [vmem] * len(rest),
        out_specs=tuple(vmem for _ in outs),
        scratch_shapes=[
            pltpu.VMEM(mats.shape, jnp.bfloat16),
            pltpu.VMEM((3 * blocks, 2 * BLK, 2 * BLK), jnp.bfloat16),
            pltpu.VMEM((rows, columns), jnp.float32),
            pltpu.SemaphoreType.DMA((mats.shape[0] // CHUNK,)),
        ],
        compiler_params=pltpu.CompilerParams(vmem_limit_bytes=VMEM_LIMIT),
        name="operator_step",
    )(dst, src, count, mats, scale, *rest)


def peer(axis, index):
    return {axis: index}


def signal_all(others):
    barrier = pltpu.get_barrier_semaphore()
    for exists, axis, index in others:
        def hello(axis=axis, index=index):
            pl.semaphore_signal(barrier, inc=1, device_id=peer(axis, index),
                                device_id_type=pl.DeviceIdType.MESH)

        if exists is None:
            hello()
        else:
            pl.when(exists)(hello)
    always = sum(exists is None for exists, _, _ in others)
    perhaps = [exists.astype(jnp.int32) for exists, _, _ in others if exists is not None]
    pl.semaphore_wait(barrier, functools.reduce(lambda x, y: x + y, perhaps, always))


def remote(src, dst, send, recv, axis, index):
    return pltpu.make_async_remote_copy(
        src_ref=src, dst_ref=dst, send_sem=send, recv_sem=recv,
        device_id=peer(axis, index), device_id_type=pl.DeviceIdType.MESH,
    )


def sides_of(count):
    me = lax.axis_index("gal")
    up = lax.rem(me + 1, count)
    down = lax.rem(me + count - 1, count)
    return me, ((me + 1 < count, up), (me > 0, down))


def swap_kernel(count, with_field, with_sums, *refs):
    refs = list(refs)
    field = refs.pop(0) if with_field else None
    sums = refs.pop(0) if with_sums else None
    outs = (refs.pop(0), refs.pop(0)) if with_field else None
    sums_out = refs.pop(0) if with_sums else None
    me, sides = sides_of(count)
    if with_sums:
        slots, sum_send, sum_recv = refs[:3]
        refs = refs[3:]
        signal_all([(None, "gal", lax.rem(me + o, count)) for o in range(1, count)])
    else:
        signal_all([(exists, "gal", index) for exists, index in sides])
    if with_sums:
        sends = [
            remote(sums, slots.at[o], sum_send.at[o], sum_recv.at[o], "gal", lax.rem(me + o, count))
            for o in range(1, count)
        ]
        for copy in sends:
            copy.start()
    if with_field:
        send, recv = refs
        copies = [
            remote(field, outs[i], send.at[i], recv.at[i], "gal", index)
            for i, (_, index) in enumerate(sides)
        ]
        for copy, (exists, _) in zip(copies, sides):
            pl.when(exists)(copy.start)
    if with_sums:
        for copy in sends:
            copy.wait()
        all_sums = sums[...]
        for o in range(1, count):
            all_sums += slots[o]
        sums_out[...] = all_sums
    if with_field:
        for i in range(2):
            pl.when(sides[i][0])(copies[i].wait_send)
            pl.when(sides[1 - i][0])(copies[i].wait_recv)


def swap(ident, field=None, sums=None):
    count = lax.axis_size("gal")
    anywhere = pl.BlockSpec(memory_space=pl.ANY)
    vmem = pl.BlockSpec(memory_space=pltpu.VMEM)
    args, specs, outs, out_specs, scratch = [], [], [], [], []
    if field is not None:
        args.append(field)
        specs.append(anywhere)
        outs += [jax.ShapeDtypeStruct(field.shape, field.dtype)] * 2
        out_specs += [anywhere] * 2
    if sums is not None:
        args.append(sums)
        specs.append(vmem)
        outs.append(jax.ShapeDtypeStruct(sums.shape, sums.dtype))
        out_specs.append(vmem)
        scratch += [
            pltpu.VMEM((count,) + sums.shape, sums.dtype),
            pltpu.SemaphoreType.DMA((count,)),
            pltpu.SemaphoreType.DMA((count,)),
        ]
    if field is not None:
        scratch += [pltpu.SemaphoreType.DMA((2,)), pltpu.SemaphoreType.DMA((2,))]
    return pl.pallas_call(
        functools.partial(swap_kernel, count, field is not None, sums is not None),
        out_shape=tuple(outs),
        in_specs=specs,
        out_specs=tuple(out_specs),
        scratch_shapes=scratch,
        compiler_params=pltpu.CompilerParams(collective_id=ident, has_side_effects=True),
        name="swap",
    )(*args)


PIECES = 8
FLIGHT = 3


def gather_kernel(count, parts, own, near, window, near_all,
                  far_send, far_recv, *level_sems):
    rows, tiles = own.shape[0], near.shape[0]
    size, tile_size = rows // parts, tiles // parts
    step, tile_step = size // PIECES, tile_size // PIECES
    part = lax.axis_index("qry")
    me, sides = sides_of(count)
    bits = [1 << b for b in reversed(range(parts.bit_length() - 1))]

    def partner(bit):
        return part + bit - 2 * bit * lax.rem(part // bit, 2)

    signal_all([(exists, "gal", index) for exists, index in sides]
               + [(None, "qry", partner(bit)) for bit in bits])

    def pair(index, piece, side):
        at = index * size + piece * step
        near_at = index * tile_size + piece * tile_step
        base = (0, rows)[side]
        near_base = (0, tiles)[side]
        return (
            (own.at[pl.ds(at, step)], window.at[pl.ds(base + at, step)]),
            (near.at[pl.ds(near_at, tile_step)], near_all.at[pl.ds(near_base + near_at, tile_step)]),
        )

    far = {}
    for piece in range(PIECES):
        for i, (_, index) in enumerate(sides):
            far[piece, i] = [
                remote(src, dst, far_send.at[piece, i, k], far_recv.at[piece, i, k], "gal", index)
                for k, (src, dst) in enumerate(pair(part, piece, i))
            ]
    def launch(piece, side):
        @pl.when(sides[side][0])
        def _():
            for copy in far[piece, side]:
                copy.start()

    for piece in range(FLIGHT):
        for side in range(2):
            launch(piece, side)

    def forward(piece, side, level):
        bit = bits[level]
        held = [part]
        for earlier in bits[:level]:
            held = held + [index + (partner(earlier) - part) for index in held]
        send, recv = level_sems[2 * level:2 * level + 2]
        return [
            remote(spot, spot, send.at[piece, side, n, k], recv.at[piece, side, n, k],
                   "qry", partner(bit))
            for n, index in enumerate(held)
            for k, (_, spot) in enumerate(pair(index, piece, side))
        ]

    order = [(piece, side) for piece in range(PIECES) for side in range(2)]
    depth = len(bits)
    for turn in range(len(order) + depth - 1):
        for level in range(depth):
            if not 0 <= turn - level < len(order):
                continue
            piece, side = order[turn - level]

            @pl.when(sides[1 - side][0])
            def _(piece=piece, side=side, level=level):
                for copy in forward(piece, side, level - 1) if level else far[piece, side]:
                    copy.wait_recv()
                for copy in forward(piece, side, level):
                    copy.start()

            if level == 0:
                @pl.when(sides[side][0])
                def _(piece=piece, side=side):
                    for copy in far[piece, side]:
                        copy.wait_send()

                if piece + FLIGHT < PIECES:
                    launch(piece + FLIGHT, side)

    for piece, side in order:
        @pl.when(sides[1 - side][0])
        def _(piece=piece, side=side):
            for copy in forward(piece, side, len(bits) - 1):
                copy.wait_recv()
            for level in range(len(bits)):
                for copy in forward(piece, side, level):
                    copy.wait_send()


def gather(own, near):
    count, parts = lax.axis_size("gal"), lax.axis_size("qry")
    anywhere = pl.BlockSpec(memory_space=pl.ANY)
    levels = []
    for level in range(parts.bit_length() - 1):
        levels += [pltpu.SemaphoreType.DMA((PIECES, 2, 1 << level, 2))] * 2
    return pl.pallas_call(
        functools.partial(gather_kernel, count, parts),
        out_shape=(
            jax.ShapeDtypeStruct((2 * own.shape[0],) + own.shape[1:], own.dtype),
            jax.ShapeDtypeStruct((2 * near.shape[0],) + near.shape[1:], near.dtype),
        ),
        in_specs=[anywhere] * 2,
        out_specs=(anywhere, anywhere),
        scratch_shapes=[
            pltpu.SemaphoreType.DMA((PIECES, 2, 2)),
            pltpu.SemaphoreType.DMA((PIECES, 2, 2)),
        ] + levels,
        compiler_params=pltpu.CompilerParams(collective_id=0, has_side_effects=True),
        name="gather_beside",
    )(own, near)


def per_device(descriptors, query_descriptors, tile_blocks, neighbours):
    rows, width = descriptors.shape
    tiles = tile_blocks.shape[0]
    blocks = rows // BLK
    place = lax.axis_index("gal")
    count = lax.axis_size("gal")
    entries = neighbours.shape[1]

    first = place * blocks
    spot = tile_blocks - jnp.stack([first, first - blocks])[None, :]
    spots = jnp.pad(spot, ((0, 0), (0, BLK - 2)))[:, None, :]
    near = jnp.concatenate([neighbours, spots], axis=1)
    near = jnp.pad(near, ((0, 0), (0, 16 - entries - 1), (0, 0))).astype(jnp.bfloat16)
    beside, near_beside = gather(descriptors, near)
    spots = near_beside[:, entries, 0:2].astype(jnp.int32)
    shift = jnp.repeat(jnp.array([-1, 1], jnp.int32), tiles)
    origin = shift + place
    exists = jnp.logical_and(origin >= 0, origin < count)
    row = jnp.concatenate([spot[:, 0] + blocks, spots[:, 0] + (1 + shift) * blocks])
    col = jnp.concatenate(
        [spot[:, 1], jnp.where(exists, spots[:, 1] + shift * blocks, jnp.int32(3 * blocks))]
    )

    mats, degree, dst, src, used = build(entries, row, col, descriptors, beside, near, near_beside)
    scale = 1.0 / jnp.sqrt(1.0 + degree)
    scale_low, scale_high = swap(1, scale[:, 0].reshape(blocks, BLK))

    def seeds(field):
        dots = lax.dot_general(field, query_descriptors, (((1,), (1,)), ((), ())),
                               preferred_element_type=jnp.float32)
        return jax.nn.softplus(dots / math.sqrt(width))

    own = seeds(descriptors)
    halo = seeds(beside) * jnp.concatenate([scale_low, scale_high]).reshape(2 * rows, 1)
    image0, sums0, send0 = run_step(0, dst, src, used, mats, scale, own, halo)
    low0, high0, sums0 = swap(2, send0, sums0)
    res1, dir1, image1, sums1, send1, halo1, tail1 = run_step(
        1, dst, src, used, mats, scale, sums0, own, own, image0, halo, low0, high0
    )
    low1, high1, sums1 = swap(2, send1, sums1)
    res2, dir2, image2, sums2 = run_step(
        2, dst, src, used, mats, scale, sums1, res1, dir1, image1, halo1, tail1, low1, high1
    )
    (sums2,) = swap(3, None, sums2)
    alpha0, alpha1, alpha2 = (s[0:1] / s[1:2] for s in (sums0, sums1, sums2))
    ranking = alpha0 * own + alpha1 * dir1 + alpha2 * dir2
    residual = res2 - alpha2 * image2
    return ranking, residual


def solution(mesh):
    placed = (P("gal", None), P("qry", None), P("gal", None), P("gal", None, None))
    return jax.shard_map(
        per_device,
        mesh=mesh,
        in_specs=placed,
        out_specs=(P("gal", "qry"), P("gal", "qry")),
        check_vma=False,
    )
```

```python
import functools
import math

import jax
import jax.numpy as jnp
from jax import lax
from jax.experimental import pallas as pl
from jax.experimental.pallas import tpu as pltpu
from jax.sharding import PartitionSpec as P

BLK = 128
DAMPING = 0.99
STAGE = 8
GROUP = 4
SHARES = 4
CHUNK = 16
VMEM_LIMIT = 60 * 1024 * 1024


def softplus(value):
    return jnp.maximum(value, 0.0) + jnp.log(1.0 + jnp.exp(-jnp.abs(value)))


def build_kernel(tiles, entries, blocks, row_ref, col_ref, own_ref, beside_ref, near_own, near_beside,
                 mats_ref, degree_ref, dst_ref, src_ref, count_ref,
                 window_ref, near_ref, stage, listed, load_sems, sems):
    size = blocks * BLK
    loads = [
        pltpu.make_async_copy(src, dst, load_sems.at[i])
        for i, (src, dst) in enumerate((
            (own_ref, window_ref.at[pl.ds(size, size)]),
            (beside_ref.at[pl.ds(0, size)], window_ref.at[pl.ds(0, size)]),
            (beside_ref.at[pl.ds(size, size)], window_ref.at[pl.ds(2 * size, size)]),
            (near_own, near_ref.at[pl.ds(0, tiles)]),
            (near_beside, near_ref.at[pl.ds(tiles, 2 * tiles)]),
        ))
    ]
    for load in loads:
        load.start()
    root = 1.0 / math.sqrt(window_ref.shape[1])
    degree_ref[...] = jnp.zeros_like(degree_ref)
    count_ref[0] = 0
    count_ref[1] = 0
    places = lax.broadcasted_iota(jnp.int32, (BLK, BLK), 0).astype(jnp.float32).astype(jnp.bfloat16)
    ones = jnp.ones((2 * BLK, BLK), jnp.bfloat16)
    one, none = jnp.bfloat16(1.0), jnp.bfloat16(0.0)

    def emit(mat, slot, dst, src):
        sent = count_ref[0]
        place = lax.rem(sent, STAGE)

        @pl.when(sent >= STAGE)
        def _():
            pltpu.make_async_copy(stage.at[place], mats_ref.at[0], sems.at[place]).wait()

        high = mat.astype(jnp.bfloat16)
        both = jnp.concatenate([high, (mat - high.astype(jnp.float32)).astype(jnp.bfloat16)], axis=1)
        stage[place] = both
        pltpu.make_async_copy(stage.at[place], mats_ref.at[slot], sems.at[place]).start()
        count_ref[0] = sent + 1
        dst_ref[slot] = dst
        src_ref[slot] = src
        rows = pl.ds(pl.multiple_of(dst * BLK, BLK), BLK)
        degree_ref[rows, :] += jnp.dot(both, ones, preferred_element_type=jnp.float32)

    def turned(t):
        left = window_ref[pl.ds(pl.multiple_of(row_ref[t] * BLK, BLK), BLK), :]
        right = window_ref[pl.ds(pl.multiple_of(col_ref[t] * BLK, BLK), BLK), :]
        dots = lax.dot_general(right, left, (((1,), (1,)), ((), ())),
                               preferred_element_type=jnp.float32)
        near = near_ref[t]
        counted = jnp.zeros((BLK, BLK), jnp.bfloat16)
        for k in range(entries):
            counted += jnp.where(places == near[k:k + 1, :], one, none)
        return counted.astype(jnp.float32) * softplus(dots * root)

    def mine(t):
        col = col_ref[t]
        return jnp.logical_and(col >= blocks, col < 2 * blocks)

    def emit_back(t, mat):
        slot = tiles + count_ref[1]
        emit(mat, slot, col_ref[t] - blocks, row_ref[t])
        count_ref[1] = slot - tiles + 1

    listed[0] = tiles

    def note(t, found):
        @pl.when(mine(t))
        def _():
            listed[found] = t

        return found + mine(t).astype(jnp.int32)

    found = lax.fori_loop(tiles, 3 * tiles, note, jnp.int32(0))
    for load in loads:
        load.wait()

    @pl.loop(0, tiles // GROUP)
    def _(g):
        ids = [g * GROUP + i for i in range(GROUP)]
        mats = [turned(t) for t in ids]
        for t, mat in zip(ids, mats):
            emit(mat.T, t, row_ref[t] - blocks, col_ref[t])
        for t, mat in zip(ids, mats):
            @pl.when(mine(t))
            def _(t=t, mat=mat):
                emit_back(t, mat)

    @pl.loop(0, pl.cdiv(found, GROUP))
    def _(g):
        at = [g * GROUP + i for i in range(GROUP)]
        ids = [listed[jnp.minimum(n, found - 1)] for n in at]
        mats = [turned(t) for t in ids]
        for n, t, mat in zip(at, ids, mats):
            @pl.when(n < found)
            def _(t=t, mat=mat):
                emit_back(t, mat)

    for place in range(STAGE):
        pltpu.make_async_copy(stage.at[place], mats_ref.at[0], sems.at[place]).wait()


def build(entries, row, col, own, beside, near, near_beside):
    tiles = near.shape[0]
    blocks = own.shape[0] // BLK
    anywhere = pl.BlockSpec(memory_space=pl.ANY)
    smem = pl.BlockSpec(memory_space=pltpu.SMEM)
    vmem = pl.BlockSpec(memory_space=pltpu.VMEM)
    return pl.pallas_call(
        functools.partial(build_kernel, tiles, entries, blocks),
        out_shape=(
            jax.ShapeDtypeStruct((4 * tiles, BLK, 2 * BLK), jnp.bfloat16),
            jax.ShapeDtypeStruct((blocks * BLK, BLK), jnp.float32),
            jax.ShapeDtypeStruct((4 * tiles,), jnp.int32),
            jax.ShapeDtypeStruct((4 * tiles,), jnp.int32),
            jax.ShapeDtypeStruct((2,), jnp.int32),
        ),
        in_specs=[smem, smem] + [anywhere] * 4,
        out_specs=(pl.BlockSpec(memory_space=pl.ANY), vmem, smem, smem, smem),
        scratch_shapes=[
            pltpu.VMEM((3 * own.shape[0],) + own.shape[1:], own.dtype),
            pltpu.VMEM((3 * tiles,) + near.shape[1:], near.dtype),
            pltpu.VMEM((STAGE, BLK, 2 * BLK), jnp.bfloat16),
            pltpu.SMEM((2 * tiles,), jnp.int32),
            pltpu.SemaphoreType.DMA((5,)),
            pltpu.SemaphoreType.DMA((STAGE,)),
        ],
        compiler_params=pltpu.CompilerParams(vmem_limit_bytes=VMEM_LIMIT),
        name="build_tiles",
    )(row, col, own, beside, near, near_beside)


def step_kernel(step, blocks, tiles, *refs):
    refs = list(refs)

    def take(count):
        taken = refs[:count]
        del refs[:count]
        return taken

    dst_ref, src_ref, count_ref, mats_ref, scale_ref = take(5)
    if step == 0:
        dir_in, halo_in = take(2)
        res_in = dir_in
    else:
        sums_in, res_in, dir_in, image_in = take(4)
        if step == 1:
            (halo_in,) = take(1)
            tail_in = halo_in
        else:
            halo_in, tail_in = take(2)
        fresh_low, fresh_high = take(2)
    if step > 0:
        res_out, dir_out = take(2)
    image_out, sums_out = take(2)
    if step < 2:
        (send_out,) = take(1)
    if step == 1:
        halo_out, tail_out = take(2)
    mats, field, total, sems = refs

    chunks = mats.shape[0] // CHUNK
    used = tiles + count_ref[1]

    def fetch(c):
        span = pl.ds(c * CHUNK, CHUNK)
        return pltpu.make_async_copy(mats_ref.at[span], mats.at[span], sems.at[c])

    for c in range(chunks):
        @pl.when(c * CHUNK < used)
        def _():
            fetch(c).start()

    total[...] = jnp.zeros_like(total)
    sums_out[...] = jnp.zeros_like(sums_out)
    if step > 0:
        norm = sums_in[0:1, :]
        alpha = norm / sums_in[1:2, :]
        after = norm - 2.0 * alpha * sums_in[2:3, :] + alpha * alpha * sums_in[3:4, :]
        beta = after / norm

    def put(block, value):
        high = value.astype(jnp.bfloat16)
        low = (value - high.astype(jnp.float32)).astype(jnp.bfloat16)
        field[block, 0:BLK, 0:BLK] = high
        field[block, 0:BLK, BLK:] = low
        field[block, BLK:, 0:BLK] = high
        field[block, BLK:, BLK:] = low

    def rows_of(b):
        return pl.ds(pl.multiple_of(b * BLK, BLK), BLK)

    @pl.loop(0, blocks)
    def _(b):
        rows = rows_of(b)
        direction = dir_in[rows, :]
        if step > 0:
            residual = res_in[rows, :] - alpha * image_in[rows, :]
            direction = residual + beta * direction
            res_out[rows, :] = residual
            dir_out[rows, :] = direction
        put(blocks + b, direction * scale_ref[rows, :])
        for half in range(2):
            here = rows_of(half * blocks + b)
            value = halo_in[here, :]
            if step > 0:
                fresh = (fresh_low, fresh_high)[half][rows, :]
                tail = tail_in[here, :] - alpha * fresh
                value = tail + beta * value
                if step == 1:
                    halo_out[here, :] = value
                    tail_out[here, :] = tail
            put(2 * half * blocks + b, value)

    def partial(n):
        both = jnp.dot(mats[n], field[src_ref[n]], preferred_element_type=jnp.float32)
        return both[:, 0:BLK] + both[:, BLK:]

    def run(first, count):
        terms = [partial(first + i) for i in range(count)]
        for i in range(count):
            total[rows_of(dst_ref[first + i]), :] += terms[i]

    @pl.loop(0, pl.cdiv(used, CHUNK))
    def _(c):
        fetch(c).wait()
        first = c * CHUNK
        have = jnp.minimum(CHUNK, used - first)

        @pl.loop(0, have // 4)
        def _(g):
            run(first + 4 * g, 4)

        @pl.loop(have // 4 * 4, have)
        def _(i):
            run(first + i, 1)

    @pl.loop(0, blocks)
    def _(b):
        rows = rows_of(b)
        scale = scale_ref[rows, :]
        direction = (dir_out if step > 0 else dir_in)[rows, :]
        residual = (res_out if step > 0 else res_in)[rows, :]
        image = direction - DAMPING * scale * total[rows, :]
        image_out[rows, :] = image
        if step < 2:
            send_out[rows, :] = scale * image
        for place, value in enumerate(
            (residual * residual, direction * image, residual * image, image * image)
        ):
            sums_out[place:place + 1, :] += jnp.sum(value, axis=0, keepdims=True)


def run_step(step, dst, src, count, mats, scale, *rest):
    rows, columns = scale.shape[0], rest[-1].shape[1]
    tiles = dst.shape[0] // 4
    blocks = rows // BLK
    smem = pl.BlockSpec(memory_space=pltpu.SMEM)
    vmem = pl.BlockSpec(memory_space=pltpu.VMEM)
    own = jax.ShapeDtypeStruct((rows, columns), jnp.float32)
    twice = jax.ShapeDtypeStruct((2 * rows, columns), jnp.float32)
    sums = jax.ShapeDtypeStruct((8, columns), jnp.float32)
    outs = ([own, own] if step > 0 else []) + [own, sums]
    if step < 2:
        outs += [own]
    if step == 1:
        outs += [twice, twice]
    return pl.pallas_call(
        functools.partial(step_kernel, step, blocks, tiles),
        out_shape=tuple(outs),
        in_specs=[smem, smem, smem, pl.BlockSpec(memory_space=pl.ANY), vmem]
        + [vmem] * len(rest),
        out_specs=tuple(vmem for _ in outs),
        scratch_shapes=[
            pltpu.VMEM(mats.shape, jnp.bfloat16),
            pltpu.VMEM((3 * blocks, 2 * BLK, 2 * BLK), jnp.bfloat16),
            pltpu.VMEM((rows, columns), jnp.float32),
            pltpu.SemaphoreType.DMA((mats.shape[0] // CHUNK,)),
        ],
        compiler_params=pltpu.CompilerParams(vmem_limit_bytes=VMEM_LIMIT),
        name="operator_step",
    )(dst, src, count, mats, scale, *rest)


def peer(axis, index):
    return {axis: index}


def signal_all(others):
    barrier = pltpu.get_barrier_semaphore()
    for exists, axis, index in others:
        def hello(axis=axis, index=index):
            pl.semaphore_signal(barrier, inc=1, device_id=peer(axis, index),
                                device_id_type=pl.DeviceIdType.MESH)

        if exists is None:
            hello()
        else:
            pl.when(exists)(hello)
    always = sum(exists is None for exists, _, _ in others)
    perhaps = [exists.astype(jnp.int32) for exists, _, _ in others if exists is not None]
    pl.semaphore_wait(barrier, functools.reduce(lambda x, y: x + y, perhaps, always))


def remote(src, dst, send, recv, axis, index):
    return pltpu.make_async_remote_copy(
        src_ref=src, dst_ref=dst, send_sem=send, recv_sem=recv,
        device_id=peer(axis, index), device_id_type=pl.DeviceIdType.MESH,
    )


def sides_of(count):
    me = lax.axis_index("gal")
    up = lax.rem(me + 1, count)
    down = lax.rem(me + count - 1, count)
    return me, ((me + 1 < count, up), (me > 0, down))


def swap_kernel(count, with_field, with_sums, *refs):
    refs = list(refs)
    field = refs.pop(0) if with_field else None
    sums = refs.pop(0) if with_sums else None
    outs = (refs.pop(0), refs.pop(0)) if with_field else None
    sums_out = refs.pop(0) if with_sums else None
    me, sides = sides_of(count)
    if with_sums:
        slots, sum_send, sum_recv = refs[:3]
        refs = refs[3:]
        signal_all([(None, "gal", lax.rem(me + o, count)) for o in range(1, count)])
    else:
        signal_all([(exists, "gal", index) for exists, index in sides])
    if with_sums:
        sends = [
            remote(sums, slots.at[o], sum_send.at[o], sum_recv.at[o], "gal", lax.rem(me + o, count))
            for o in range(1, count)
        ]
        for copy in sends:
            copy.start()
    if with_field:
        send, recv = refs
        shares = send.shape[1]
        length = field.shape[0] // shares
        copies = {
            (i, n): remote(field.at[pl.ds(n * length, length)], outs[i].at[pl.ds(n * length, length)],
                           send.at[i, n], recv.at[i, n], "gal", index)
            for n in range(shares)
            for i, (_, index) in enumerate(sides)
        }
        for (i, _), copy in copies.items():
            pl.when(sides[i][0])(copy.start)
    if with_sums:
        for copy in sends:
            copy.wait()
        all_sums = sums[...]
        for o in range(1, count):
            all_sums += slots[o]
        sums_out[...] = all_sums
    if with_field:
        for (i, _), copy in copies.items():
            pl.when(sides[i][0])(copy.wait_send)
            pl.when(sides[1 - i][0])(copy.wait_recv)


def swap(ident, field=None, sums=None):
    count = lax.axis_size("gal")
    anywhere = pl.BlockSpec(memory_space=pl.ANY)
    vmem = pl.BlockSpec(memory_space=pltpu.VMEM)
    args, specs, outs, out_specs, scratch = [], [], [], [], []
    if field is not None:
        args.append(field)
        specs.append(anywhere)
        outs += [jax.ShapeDtypeStruct(field.shape, field.dtype)] * 2
        out_specs += [anywhere] * 2
    if sums is not None:
        args.append(sums)
        specs.append(vmem)
        outs.append(jax.ShapeDtypeStruct(sums.shape, sums.dtype))
        out_specs.append(vmem)
        scratch += [
            pltpu.VMEM((count,) + sums.shape, sums.dtype),
            pltpu.SemaphoreType.DMA((count,)),
            pltpu.SemaphoreType.DMA((count,)),
        ]
    if field is not None:
        shares = SHARES if field.shape[0] % (SHARES * BLK) == 0 else 1
        scratch += [pltpu.SemaphoreType.DMA((2, shares)), pltpu.SemaphoreType.DMA((2, shares))]
    return pl.pallas_call(
        functools.partial(swap_kernel, count, field is not None, sums is not None),
        out_shape=tuple(outs),
        in_specs=specs,
        out_specs=tuple(out_specs),
        scratch_shapes=scratch,
        compiler_params=pltpu.CompilerParams(collective_id=ident, has_side_effects=True),
        name="swap",
    )(*args)


PIECES = 8
FLIGHT = 3


def gather_kernel(count, parts, own, near, window, near_all,
                  far_send, far_recv, *level_sems):
    rows, tiles = own.shape[0], near.shape[0]
    size, tile_size = rows // parts, tiles // parts
    step, tile_step = size // PIECES, tile_size // PIECES
    part = lax.axis_index("qry")
    me, sides = sides_of(count)
    bits = [1 << b for b in reversed(range(parts.bit_length() - 1))]

    def partner(bit):
        return part + bit - 2 * bit * lax.rem(part // bit, 2)

    signal_all([(exists, "gal", index) for exists, index in sides]
               + [(None, "qry", partner(bit)) for bit in bits])

    def pair(index, piece, side):
        at = index * size + piece * step
        near_at = index * tile_size + piece * tile_step
        base = (0, rows)[side]
        near_base = (0, tiles)[side]
        return (
            (own.at[pl.ds(at, step)], window.at[pl.ds(base + at, step)]),
            (near.at[pl.ds(near_at, tile_step)], near_all.at[pl.ds(near_base + near_at, tile_step)]),
        )

    far = {}
    for piece in range(PIECES):
        for i, (_, index) in enumerate(sides):
            far[piece, i] = [
                remote(src, dst, far_send.at[piece, i, k], far_recv.at[piece, i, k], "gal", index)
                for k, (src, dst) in enumerate(pair(part, piece, i))
            ]
    def launch(piece, side):
        @pl.when(sides[side][0])
        def _():
            for copy in far[piece, side]:
                copy.start()

    for piece in range(FLIGHT):
        for side in range(2):
            launch(piece, side)

    def forward(piece, side, level):
        bit = bits[level]
        held = [part]
        for earlier in bits[:level]:
            held = held + [index + (partner(earlier) - part) for index in held]
        send, recv = level_sems[2 * level:2 * level + 2]
        return [
            remote(spot, spot, send.at[piece, side, n, k], recv.at[piece, side, n, k],
                   "qry", partner(bit))
            for n, index in enumerate(held)
            for k, (_, spot) in enumerate(pair(index, piece, side))
        ]

    order = [(piece, side) for piece in range(PIECES) for side in range(2)]
    depth = len(bits)
    for turn in range(len(order) + depth - 1):
        for level in range(depth):
            if not 0 <= turn - level < len(order):
                continue
            piece, side = order[turn - level]

            @pl.when(sides[1 - side][0])
            def _(piece=piece, side=side, level=level):
                for copy in forward(piece, side, level - 1) if level else far[piece, side]:
                    copy.wait_recv()
                for copy in forward(piece, side, level):
                    copy.start()

            if level == 0:
                @pl.when(sides[side][0])
                def _(piece=piece, side=side):
                    for copy in far[piece, side]:
                        copy.wait_send()

                if piece + FLIGHT < PIECES:
                    launch(piece + FLIGHT, side)

    for piece, side in order:
        @pl.when(sides[1 - side][0])
        def _(piece=piece, side=side):
            for copy in forward(piece, side, len(bits) - 1):
                copy.wait_recv()
            for level in range(len(bits)):
                for copy in forward(piece, side, level):
                    copy.wait_send()


def gather(own, near):
    count, parts = lax.axis_size("gal"), lax.axis_size("qry")
    anywhere = pl.BlockSpec(memory_space=pl.ANY)
    levels = []
    for level in range(parts.bit_length() - 1):
        levels += [pltpu.SemaphoreType.DMA((PIECES, 2, 1 << level, 2))] * 2
    return pl.pallas_call(
        functools.partial(gather_kernel, count, parts),
        out_shape=(
            jax.ShapeDtypeStruct((2 * own.shape[0],) + own.shape[1:], own.dtype),
            jax.ShapeDtypeStruct((2 * near.shape[0],) + near.shape[1:], near.dtype),
        ),
        in_specs=[anywhere] * 2,
        out_specs=(anywhere, anywhere),
        scratch_shapes=[
            pltpu.SemaphoreType.DMA((PIECES, 2, 2)),
            pltpu.SemaphoreType.DMA((PIECES, 2, 2)),
        ] + levels,
        compiler_params=pltpu.CompilerParams(collective_id=0, has_side_effects=True),
        name="gather_beside",
    )(own, near)


def per_device(descriptors, query_descriptors, tile_blocks, neighbours):
    rows, width = descriptors.shape
    tiles = tile_blocks.shape[0]
    blocks = rows // BLK
    place = lax.axis_index("gal")
    count = lax.axis_size("gal")
    entries = neighbours.shape[1]

    first = place * blocks
    spot = tile_blocks - jnp.stack([first, first - blocks])[None, :]
    spots = jnp.pad(spot, ((0, 0), (0, BLK - 2)))[:, None, :]
    near = jnp.concatenate([neighbours, spots], axis=1)
    near = jnp.pad(near, ((0, 0), (0, 16 - entries - 1), (0, 0))).astype(jnp.bfloat16)
    beside, near_beside = gather(descriptors, near)
    spots = near_beside[:, entries, 0:2].astype(jnp.int32)
    shift = jnp.repeat(jnp.array([-1, 1], jnp.int32), tiles)
    origin = shift + place
    exists = jnp.logical_and(origin >= 0, origin < count)
    row = jnp.concatenate([spot[:, 0] + blocks, spots[:, 0] + (1 + shift) * blocks])
    col = jnp.concatenate(
        [spot[:, 1], jnp.where(exists, spots[:, 1] + shift * blocks, jnp.int32(3 * blocks))]
    )

    mats, degree, dst, src, used = build(entries, row, col, descriptors, beside, near, near_beside)
    scale = 1.0 / jnp.sqrt(1.0 + degree)
    scale_low, scale_high = swap(1, scale[:, 0].reshape(blocks, BLK))

    def seeds(field):
        dots = lax.dot_general(field, query_descriptors, (((1,), (1,)), ((), ())),
                               preferred_element_type=jnp.float32)
        return jax.nn.softplus(dots / math.sqrt(width))

    own = seeds(descriptors)
    halo = seeds(beside) * jnp.concatenate([scale_low, scale_high]).reshape(2 * rows, 1)
    image0, sums0, send0 = run_step(0, dst, src, used, mats, scale, own, halo)
    low0, high0, sums0 = swap(2, send0, sums0)
    res1, dir1, image1, sums1, send1, halo1, tail1 = run_step(
        1, dst, src, used, mats, scale, sums0, own, own, image0, halo, low0, high0
    )
    low1, high1, sums1 = swap(2, send1, sums1)
    res2, dir2, image2, sums2 = run_step(
        2, dst, src, used, mats, scale, sums1, res1, dir1, image1, halo1, tail1, low1, high1
    )
    (sums2,) = swap(3, None, sums2)
    alpha0, alpha1, alpha2 = (s[0:1] / s[1:2] for s in (sums0, sums1, sums2))
    ranking = alpha0 * own + alpha1 * dir1 + alpha2 * dir2
    residual = res2 - alpha2 * image2
    return ranking, residual


def solution(mesh):
    placed = (P("gal", None), P("qry", None), P("gal", None), P("gal", None, None))
    return jax.shard_map(
        per_device,
        mesh=mesh,
        in_specs=placed,
        out_specs=(P("gal", "qry"), P("gal", "qry")),
        check_vma=False,
    )
```
